32 devices in a mesh: groups: 2 (over x), slab: 16 (over z, y, core).
Axes of the slice: x: 2, y: 2, z: 4, core: 2. Of those that a mesh axis runs over, the one named last changes fastest.
Arguments:
- volume: bfloat16 [32, 128, 80, 256], P(None, ('groups', 'slab')), parts along dimension 1, may hold values from -6 to 6
- weights: bfloat16 [3, 3, 3, 32, 64], replicated, may hold values from -0.21875 to 0.21875
- bias: float32 [64], replicated, may hold values from -4 to 4
- upstream: bfloat16 [64, 64, 40, 128], P(None, ('groups', 'slab')), parts along dimension 1, may hold values from -6 to 6
Outputs:
- input_grad: bfloat16 [32, 128, 80, 256], P(None, ('groups', 'slab')), parts along dimension 1
- weight_grad: float32 [6, 3, 3, 32, 64], P('groups'), parts along dimension 0
- bias_grad: float32 [128], P('groups'), parts along dimension 0
The draws below stay inside these ranges and needn't reach their ends.
There are 2 independent parts, one for each index of `groups`. The reference program is written for one: setup_inputs(seed, part) draws one part's arguments, and reference() takes and returns one part's arrays. A program takes and returns all parts, laid end to end along the dimension named above; an argument that names none is the same for every part. Nothing has to cross between parts.
All inputs are finite; a program needn't handle non-finite values.
Results may differ from the reference program's by a relative error of at most 0.005.
Values may be sent and summed in bfloat16 or wider, within the bound.
No kernel may reach another device: no remote copies, remote signals or barrier semaphores. Data moves between devices by JAX's collectives and lax.ppermute only.
A program may use at most 192 MiB of HBM per device.

```python
import jax
import jax.numpy as jnp
from jax import lax

CIN = 32
COUT = 64
NY = 80
NX = 256
NZ = 64


def level_of(key, dims, cuts, low, largest):
    def one(position, blocks):
        steps = jax.random.uniform(jax.random.fold_in(jax.random.fold_in(key, 6), position), (blocks,), jnp.float32, low / len(cuts), largest / len(cuts))
        return jnp.repeat(jnp.exp(steps), dims[position] // blocks).reshape((-1,) + (1,) * (len(dims) - position - 1))

    level = one(*cuts[0])
    for cut in cuts[1:]:
        level = level * one(*cut)
    return level


def normal_values(key, shape, width, most, cuts=(), held_as=jnp.bfloat16):
    values = width * jax.random.normal(key, shape, jnp.float32)
    if cuts:
        values = values * level_of(key, shape, cuts, -0.22, 0.18)
    return jnp.clip(values, -most, most).astype(held_as)


def setup_inputs(seed: int = 0, part: int = 0) -> dict:
    splits = jax.random.split(jax.random.key(seed), 5)
    part_keys = jax.random.split(jax.random.fold_in(splits[4], part), 5)
    volume = normal_values(part_keys[0], (CIN, NZ, NY, NX), 1.0, 6.0, ((1, 16),))
    weights = normal_values(splits[1], (3, 3, 3, CIN, COUT), (27 * CIN) ** -0.5, 0.21875)
    bias = normal_values(splits[2], (COUT,), 1.0, 4.0, (), jnp.float32)
    upstream = normal_values(part_keys[3], (COUT, NZ // 2, NY // 2, NX // 2), 1.0, 6.0, ((1, 16),))
    return dict(volume=volume, weights=weights, bias=bias, upstream=upstream)


def convolve(field, kernel):
    return lax.conv_general_dilated(field, kernel, (2, 2, 2), ((1, 1), (1, 1), (1, 1)), dimension_numbers=('NCDHW', 'DHWIO', 'NCDHW'), precision=lax.Precision.HIGHEST)

def reference(volume, weights, bias, upstream):
    field = volume.astype(jnp.float32)[None]
    kernel = weights.astype(jnp.float32)
    pre = convolve(field, kernel)[0] + bias.astype(jnp.float32)[:, None, None, None]
    slope = 0.2 + 0.8 * jax.nn.sigmoid(pre)
    pre_grad = (upstream.astype(jnp.float32) * slope).astype(jnp.bfloat16)
    _, pull = jax.vjp(convolve, field, kernel)
    field_grad, weight_grad = pull(pre_grad.astype(jnp.float32)[None])
    bias_grad = lax.optimization_barrier(jnp.sum(pre_grad.astype(jnp.float32), axis=(1, 2, 3)))
    return (field_grad[0].astype(jnp.bfloat16), weight_grad, bias_grad)
```

```python
import functools

import jax
import jax.numpy as jnp
from jax import lax
from jax.experimental import pallas as pl
from jax.experimental.pallas import tpu as pltpu
from jax.sharding import PartitionSpec as P

BF = jnp.bfloat16
F32 = jnp.float32
VMEM = pl.BlockSpec(memory_space=pltpu.VMEM)
PARAMS = pltpu.CompilerParams(vmem_limit_bytes=50 * 2**20)


def shape(*dims, dtype=BF):
    return jax.ShapeDtypeStruct(dims, dtype)


def cost(flops, size):
    return pl.CostEstimate(flops=flops, bytes_accessed=size, transcendentals=0)


def picks(half, inverse):
    if inverse:
        row = lax.broadcasted_iota(jnp.int32, (2 * half, 2 * half), 0)
        col = lax.broadcasted_iota(jnp.int32, (2 * half, 2 * half), 1)
        hit = jnp.where(row < half, 2 * row, 2 * (row - half) + 1) == col
    else:
        row = lax.broadcasted_iota(jnp.int32, (2 * half, 3 * half), 0)
        col = lax.broadcasted_iota(jnp.int32, (2 * half, 3 * half), 1)
        early = 2 * col - 1
        even = 2 * (col - half)
        odd = 2 * (col - 2 * half) + 1
        hit = jnp.where(col < half, early, jnp.where(col < 2 * half, even, odd)) == row
    return jnp.where(hit, 1.0, 0.0).astype(BF)


def split_plane(read, lines, table):
    rows, channels, half = lines.shape
    channels //= 3
    lines[0] = jnp.zeros((3 * channels, half), BF)

    def step(t, carry):
        block = jnp.swapaxes(read(pl.multiple_of(t * 16, 16)), 0, 1)
        flat = block.reshape(16 * channels, 2 * half)
        taps = jnp.dot(flat, table, preferred_element_type=F32).astype(BF)
        taps = taps.reshape(16, channels, 3 * half)
        for e in range(3):
            lines[pl.ds(1 + t * 16, 16), e * channels : (e + 1) * channels, :] = taps[
                :, :, e * half : (e + 1) * half
            ]
        return carry

    lax.fori_loop(0, (rows - 1) // 16, step, 0)


def turn_upstream(upstream, turned):
    for o in range(0, upstream.shape[0], 8):
        block = upstream[o : o + 8].astype(F32)
        turned[:, o : o + 8, :] = jnp.swapaxes(block, 0, 1)


def earlier(values):
    cells = values.shape[-1]
    lane = lax.broadcasted_iota(jnp.int32, values.shape, values.ndim - 1)
    return jnp.where(lane == cells - 1, 0.0, pltpu.roll(values, cells - 1, values.ndim - 1))


def store_grads(pre, upstream, grads, j):
    slope = 0.2 + 0.8 * jax.nn.sigmoid(pre)
    value = (upstream * slope).astype(BF)
    cout = value.shape[0]
    grads[j, :cout, :] = value
    grads[j, cout:, :] = earlier(value.astype(F32)).astype(BF)


def window(planes, j, count):
    parts = [plane[pl.ds(2 * j, count)].reshape(-1, plane.shape[-1]) for plane in planes]
    return parts[0] if len(parts) == 1 else jnp.concatenate(parts, 0)


def weight_terms(planes, grads):
    cells = grads.shape[-1]
    cout = grads.shape[1] // 2
    left, right = [], []
    ones = jnp.ones((16, cells), BF)
    for j in range(grads.shape[0] - 1):
        lines = [p[1 + 2 * j : 3 + 2 * j].reshape(-1, cells) for p in planes]
        left.append(jnp.concatenate(lines + [ones], 0))
        right.append(jnp.concatenate([grads[j, :cout], grads[j + 1, :cout]], 0))
    return lax.dot_general(
        jnp.concatenate(left, 1),
        jnp.concatenate(right, 1),
        (((1,), (1,)), ((), ())),
        preferred_element_type=F32,
    )


def first_kernel(
    volume, weights, bias, upstream,
    lines_out, pre_out, grads, terms, back, front,
    extra, turned, turned_weights,
):
    cin, depth = volume.shape[0], volume.shape[1]
    cout = bias.shape[0]
    half = volume.shape[3] // 2
    ny = upstream.shape[2]
    table = picks(half, False)
    planes = [lines_out.at[0], lines_out.at[1], extra.at[0], extra.at[1]]
    for z in range(4):
        split_plane(lambda y, z=z: volume[:, z, pl.ds(y, 16), :], planes[z], table)
    for a in range(3):
        for b in range(3):
            block = jnp.concatenate([weights[a, b, e] for e in range(3)], 0)
            turned_weights[:, a, b * 3 * cin : (b + 1) * 3 * cin] = block.T
    front[...] = turned_weights[:, 0, :]
    blank = jnp.zeros((cin, cout), BF)
    for a in range(3):
        for px in range(2):
            for py in range(2):
                row = []
                for dy in range(2):
                    for dx in range(2):
                        b, e = py + 1 - 2 * dy, px + 1 - 2 * dx
                        row.append(weights[a, b, e] if b >= 0 and e >= 0 else blank)
                at = (px * 2 + py) * cin
                back[a, at : at + cin, :] = jnp.concatenate(row, 1)
    turn_upstream(upstream.at[:, 1], turned)
    full = jnp.concatenate([turned_weights[:, a, :] for a in range(3)], 1)
    late = jnp.concatenate([turned_weights[:, a, :] for a in (1, 2)], 1)
    offset = bias[...]

    def upper(t, carry):
        field = jnp.concatenate([window(planes[1:], t * 8 + q, 3) for q in range(8)], 1)
        pre = jnp.dot(full, field, preferred_element_type=F32)
        for q in range(8):
            j = t * 8 + q
            store_grads(pre[:, q * half : (q + 1) * half] + offset, turned[j], grads, j)
        return carry

    def lower(t, carry):
        field = jnp.concatenate([window(planes[:2], t * 8 + q, 3) for q in range(8)], 1)
        pre = jnp.dot(late, field, preferred_element_type=F32)
        for q in range(8):
            pre_out[t * 8 + q] = pre[:, q * half : (q + 1) * half] + offset
        return carry

    lax.fori_loop(0, ny // 8, upper, 0)
    grads[ny] = jnp.zeros(grads.shape[1:], BF)
    terms[...] = weight_terms(planes[1:], grads)
    lax.fori_loop(0, ny // 8, lower, 0)


def second_kernel(
    halo, lines, pre_in, upstream, front, terms_in,
    grads, packed,
    below, turned,
):
    half = below.shape[-1]
    cout = front.shape[0]
    ny = pre_in.shape[0]
    table = picks(half, False)
    split_plane(lambda y: halo[:, 0, pl.ds(y, 16), :], below, table)
    turn_upstream(upstream.at[:, 0], turned)

    def body(t, carry):
        field = jnp.concatenate([window([below], t * 8 + q, 3) for q in range(8)], 1)
        pre = jnp.dot(front[...], field, preferred_element_type=F32)
        for q in range(8):
            j = t * 8 + q
            store_grads(pre[:, q * half : (q + 1) * half] + pre_in[j], turned[j], grads, j)
        return carry

    lax.fori_loop(0, ny // 8, body, 0)
    grads[ny] = jnp.zeros(grads.shape[1:], BF)
    terms = terms_in[...] + weight_terms([below, lines.at[0], lines.at[1]], grads)
    count = below.shape[1]
    for a in range(3):
        packed[a * count : (a + 1) * count] = terms[(2 * a + 1) * count : (2 * a + 2) * count]
    middle = jnp.concatenate([terms[2 * a * count : (2 * a + 1) * count, :cout] for a in range(3)], 0)
    rows = middle.shape[0] // 2
    packed[3 * count : 3 * count + rows] = jnp.concatenate([middle[:rows], middle[rows:]], 1)
    packed[3 * count + rows :] = jnp.concatenate(
        [terms[6 * count :][:, :cout], jnp.zeros((16, cout), F32)], 1
    )


def finish_kernel(packed, weight_grad, bias_grad):
    count = weight_grad.shape[2]
    cout = weight_grad.shape[3]
    for a in range(3):
        block = packed[a * count : (a + 1) * count]
        weight_grad[a, 2] = block[:, :cout]
        weight_grad[a, 0] = block[:, cout:]
    rows = 3 * count // 2
    middle = packed[3 * count : 3 * count + rows]
    middle = jnp.concatenate([middle[:, :cout], middle[:, cout:]], 0)
    for a in range(3):
        weight_grad[a, 1] = middle[a * count : (a + 1) * count]
    bias_grad[...] = packed[3 * count + rows :][:1, :cout]


def back_kernel(odd, fresh, aliased, *refs):
    refs = refs[1:] if aliased else refs
    if odd:
        back, grads, above, out = refs[:4]
        left = jnp.concatenate([back[2], back[0]], 1)
    else:
        back, grads, out = refs[:3]
        left = back[1]
    if fresh:
        shifted = refs[4]
        cout = above.shape[1]
        shifted[:, :cout, :] = above[...]
        shifted[:, cout:, :] = earlier(above[...].astype(F32)).astype(BF)
        above = None
    cin = out.shape[0]
    half = out.shape[3] // 2
    ny = grads.shape[0] - 1
    table = picks(half, True)

    def pair(ref, j):
        return ref[pl.ds(j, 2)].reshape(-1, half)

    def step(t, carry):
        columns = []
        for q in range(8):
            j = t * 8 + q
            parts = [pair(grads, j)]
            if fresh:
                parts.append(shifted[j])
                nxt = shifted[jnp.minimum(j + 1, ny - 1)]
                parts.append(nxt if q < 7 else jnp.where(j + 1 < ny, nxt, jnp.zeros_like(nxt)))
            elif odd:
                parts.append(pair(above, j))
            columns.append(jnp.concatenate(parts, 0))
        total = jnp.dot(left, jnp.concatenate(columns, 1), preferred_element_type=F32)
        total = total.astype(BF)
        rows = []
        for q in range(8):
            for py in range(2):
                lanes = slice(q * half, (q + 1) * half)
                even = total[py * cin : (py + 1) * cin, lanes]
                odds = total[(2 + py) * cin : (3 + py) * cin, lanes]
                rows.append(jnp.concatenate([even, odds], 1))
        merged = jnp.dot(jnp.concatenate(rows, 0), table, preferred_element_type=F32)
        merged = merged.astype(BF).reshape(16, cin, 2 * half)
        out[:, 0, pl.ds(pl.multiple_of(t * 16, 16), 16), :] = jnp.swapaxes(merged, 0, 1)
        return carry

    lax.fori_loop(0, ny // 8, step, 0)


def back_plane(z, total, full, back, grads, above=None, fresh=False):
    cin, depth, height, width = full
    args = [back, grads] + ([above] if above is not None else [])
    aliased = total is not None
    specs = [pl.BlockSpec(a.shape, lambda g, n=a.ndim: (0,) * n) for a in args]
    if aliased:
        args = [total] + args
        specs = [pl.BlockSpec(memory_space=pl.ANY)] + specs
    scratch = [pltpu.VMEM((above.shape[0], 2 * above.shape[1], above.shape[2]), BF)] if fresh else []
    return pl.pallas_call(
        functools.partial(back_kernel, above is not None, fresh, aliased),
        grid=(1,),
        in_specs=specs,
        out_specs=pl.BlockSpec((cin, 1, height, width), lambda g: (0, z, 0, 0)),
        out_shape=shape(*full),
        scratch_shapes=scratch,
        input_output_aliases={0: 0} if aliased else {},
        compiler_params=PARAMS,
        cost_estimate=cost(4 * 10**9, 4 * 2**20),
    )(*args)


def all_sum(value, axis):
    peers = lax.axis_size(axis)
    if peers & (peers - 1):
        return lax.psum(value, axis)
    if peers == 1:
        return value
    swap = [(i, i ^ 1) for i in range(peers)]
    odd = lax.axis_index(axis) & 1
    rows = value.shape[0] // 2
    halves = value.reshape(2, rows, value.shape[1])
    mine = lax.dynamic_index_in_dim(halves, odd, 0, False)
    other = lax.dynamic_index_in_dim(halves, 1 - odd, 0, False)
    mine = mine + lax.ppermute(other, axis, swap)
    step = 2
    while step < peers:
        mine = mine + lax.ppermute(mine, axis, [(i, i ^ step) for i in range(peers)])
        step *= 2
    other = lax.ppermute(mine, axis, swap)
    low = jnp.where(odd == 0, mine, other)
    high = jnp.where(odd == 0, other, mine)
    return jnp.concatenate([low, high], 0)


def shifted(x, axis, by):
    peers = lax.axis_size(axis)
    pairs = [(i, i + by) for i in range(peers) if 0 <= i + by < peers]
    return lax.ppermute(x, axis, pairs)


def shards(volume, weights, bias, upstream):
    cin, depth, height, width = volume.shape
    cout = bias.shape[0]
    ny, half = height // 2, width // 2
    rows, count = height + 1, 3 * cin
    halo = shifted(volume[:, depth - 1 :], "slab", 1)
    lines, pre, upper, terms, back, front = pl.pallas_call(
        first_kernel,
        in_specs=[VMEM] * 4,
        out_specs=[VMEM] * 6,
        out_shape=[
            shape(2, rows, count, half),
            shape(ny, cout, half, dtype=F32),
            shape(ny + 1, 2 * cout, half),
            shape(6 * count + 16, 2 * cout, dtype=F32),
            shape(3, 4 * cin, 4 * cout),
            shape(cout, 3 * count),
        ],
        scratch_shapes=[
            pltpu.VMEM((2, rows, count, half), BF),
            pltpu.VMEM((ny, cout, half), F32),
            pltpu.VMEM((cout, 3, 3 * count), BF),
        ],
        compiler_params=PARAMS,
        cost_estimate=cost(10 * 10**9, 20 * 2**20),
    )(volume, weights, bias.reshape(cout, 1), upstream)
    full = volume.shape
    total = back_plane(2, None, full, back, upper)
    total, halo = lax.optimization_barrier((total, halo))
    lower, packed = pl.pallas_call(
        second_kernel,
        in_specs=[VMEM] * 6,
        out_specs=[VMEM] * 2,
        out_shape=[
            shape(ny + 1, 2 * cout, half),
            shape(9 * count // 2 + 16, 2 * cout, dtype=F32),
        ],
        scratch_shapes=[
            pltpu.VMEM((rows, count, half), BF),
            pltpu.VMEM((ny, cout, half), F32),
        ],
        compiler_params=PARAMS,
        cost_estimate=cost(5 * 10**9, 10 * 2**20),
    )(halo, lines, pre, upstream, front, terms)
    above = shifted(lower[:ny, :cout], "slab", -1)
    packed = all_sum(packed, "slab")
    total = back_plane(0, total, full, back, lower)
    total = back_plane(1, total, full, back, lower, upper)
    total = back_plane(3, total, full, back, upper, above, True)
    weight_grad, bias_grad = pl.pallas_call(
        finish_kernel,
        in_specs=[VMEM],
        out_specs=[VMEM] * 2,
        out_shape=[shape(3, 3, count, cout, dtype=F32), shape(1, cout, dtype=F32)],
        compiler_params=PARAMS,
    )(packed)
    return (
        total,
        weight_grad.reshape(3, 3, 3, cin, cout),
        bias_grad.reshape(cout),
    )


def solution(mesh):
    placed = (
        P(None, ("groups", "slab"), None, None),
        P(),
        P(),
        P(None, ("groups", "slab"), None, None),
    )
    return jax.shard_map(
        shards,
        mesh=mesh,
        in_specs=placed,
        out_specs=(
            P(None, ("groups", "slab"), None, None),
            P("groups", None, None, None, None),
            P("groups"),
        ),
        check_vma=False,
    )
```

```python
import functools

import jax
import jax.numpy as jnp
from jax import lax
from jax.experimental import pallas as pl
from jax.experimental.pallas import tpu as pltpu
from jax.sharding import PartitionSpec as P

BF = jnp.bfloat16
F32 = jnp.float32
VMEM = pl.BlockSpec(memory_space=pltpu.VMEM)
ANY = pl.BlockSpec(memory_space=pl.ANY)
PARAMS = pltpu.CompilerParams(vmem_limit_bytes=40 * 2**20)


def shape(*dims, dtype=BF):
    return jax.ShapeDtypeStruct(dims, dtype)


def cost(flops, size):
    return pl.CostEstimate(flops=flops, bytes_accessed=size, transcendentals=0)


def picks(half, inverse):
    if inverse:
        row = lax.broadcasted_iota(jnp.int32, (2 * half, 2 * half), 0)
        col = lax.broadcasted_iota(jnp.int32, (2 * half, 2 * half), 1)
        hit = jnp.where(row < half, 2 * row, 2 * (row - half) + 1) == col
    else:
        row = lax.broadcasted_iota(jnp.int32, (2 * half, 3 * half), 0)
        col = lax.broadcasted_iota(jnp.int32, (2 * half, 3 * half), 1)
        early = 2 * col - 1
        even = 2 * (col - half)
        odd = 2 * (col - 2 * half) + 1
        hit = jnp.where(col < half, early, jnp.where(col < 2 * half, even, odd)) == row
    return jnp.where(hit, 1.0, 0.0).astype(BF)


def split_plane(read, lines, table):
    rows, channels, half = lines.shape
    channels //= 3

    def step(t, carry):
        block = jnp.swapaxes(read(pl.multiple_of(t * 16, 16)), 0, 1)
        flat = block.reshape(16 * channels, 2 * half)
        taps = jnp.dot(flat, table, preferred_element_type=F32).astype(BF)
        taps = taps.reshape(16, channels, 3 * half)
        for e in range(3):
            lines[pl.ds(1 + t * 16, 16), e * channels : (e + 1) * channels, :] = taps[
                :, :, e * half : (e + 1) * half
            ]
        return carry

    lax.fori_loop(0, (rows - 1) // 16, step, 0, unroll=True)


def turn_upstream(upstream, turned):
    for o in range(0, upstream.shape[0], 8):
        block = upstream[o : o + 8].astype(F32)
        turned[:, o : o + 8, :] = jnp.swapaxes(block, 0, 1).astype(turned.dtype)


def earlier(values):
    cells = values.shape[-1]
    lane = lax.broadcasted_iota(jnp.int32, values.shape, values.ndim - 1)
    return jnp.where(lane == cells - 1, 0.0, pltpu.roll(values, cells - 1, values.ndim - 1))


def store_grads(pre, upstream, grads, j):
    slope = 0.6 + 0.4 * jnp.tanh(0.5 * pre)
    value = (upstream * slope).astype(BF)
    cout = value.shape[0]
    grads[j, :cout, :] = value
    grads[j, cout:, :] = earlier(value.astype(F32)).astype(BF)


def window(planes, j, count):
    parts = [plane[2 * j : 2 * j + count].reshape(-1, plane.shape[-1]) for plane in planes]
    return parts[0] if len(parts) == 1 else jnp.concatenate(parts, 0)


def weight_terms(cells):
    left, right = [], []
    for lines, grads in cells:
        flat = [line.reshape(-1, line.shape[-1]) for line in lines]
        ones = jnp.ones((16, flat[0].shape[-1]), BF)
        left.append(jnp.concatenate(flat + [ones], 0))
        right.append(jnp.concatenate(grads, 0))
    return lax.dot_general(
        jnp.concatenate(left, 1),
        jnp.concatenate(right, 1),
        (((1,), (1,)), ((), ())),
        preferred_element_type=F32,
    )


class Copies:
    def __init__(self, semaphores):
        self.semaphores, self.used, self.pending = semaphores, 0, []

    def start(self, source, target):
        copy = pltpu.make_async_copy(source, target, self.semaphores.at[self.used])
        self.used += 1
        copy.start()
        self.pending.append(copy)
        return copy

    def wait(self, *copies):
        for copy in copies or list(self.pending):
            copy.wait()
            self.pending.remove(copy)


def spans(total, size):
    return [(at, min(at + size, total)) for at in range(0, total, size)]


def first_kernel(
    volume, weights, bias, upstream,
    lines_out, pre_out, turned_out, grads_out, terms, back, front,
    field, lines, inputs, turned, turned_late, pre, grads, turned_weights, semaphores,
):
    cin = volume.shape[0]
    cout = bias.shape[0]
    half = volume.shape[3] // 2
    ny = upstream.shape[2]
    copies = Copies(semaphores)
    ins = [copies.start(volume.at[:, z], field.at[z]) for z in range(2)]
    ups = [copies.start(upstream.at[:, k], inputs.at[k]) for k in range(2)]
    ins += [copies.start(volume.at[:, z], field.at[z]) for z in range(2, 4)]
    table = picks(half, False)
    planes = [lines.at[z] for z in range(4)]
    for a in range(3):
        for b in range(3):
            block = jnp.concatenate([weights[a, b, e] for e in range(3)], 0)
            turned_weights[:, a, b * 3 * cin : (b + 1) * 3 * cin] = block.T
    front[...] = turned_weights[:, 0, :]
    blank = jnp.zeros((cin, cout), BF)
    for a in range(3):
        for px in range(2):
            for py in range(2):
                row = []
                for dy in range(2):
                    for dx in range(2):
                        b, e = py + 1 - 2 * dy, px + 1 - 2 * dx
                        row.append(weights[a, b, e] if b >= 0 and e >= 0 else blank)
                at = (px * 2 + py) * cin
                back[a, at : at + cin, :] = jnp.concatenate(row, 1)
    full = jnp.concatenate([turned_weights[:, a, :] for a in range(3)], 1)
    late = jnp.concatenate([turned_weights[:, a, :] for a in (1, 2)], 1)
    offset = bias[...]

    def split(z):
        planes[z][0] = jnp.zeros(planes[z].shape[1:], BF)
        copies.wait(ins[z])
        split_plane(lambda y: field[z, :, pl.ds(y, 16), :], planes[z], table)

    for z in range(2):
        split(z)
        copies.start(lines.at[z], lines_out.at[z])
    for lo, hi in spans(ny, 8):
        block = jnp.concatenate([window(planes[:2], j, 3) for j in range(lo, hi)], 1)
        sums = jnp.dot(late, block, preferred_element_type=F32)
        for j in range(lo, hi):
            pre[j] = sums[:, (j - lo) * half : (j - lo + 1) * half] + offset
    copies.start(pre, pre_out)
    copies.wait(*ups)
    turn_upstream(inputs.at[0], turned_late)
    copies.start(turned_late, turned_out)
    turn_upstream(inputs.at[1], turned)
    for z in range(2, 4):
        split(z)
    for lo, hi in spans(ny, 8):
        block = jnp.concatenate([window(planes[1:], j, 3) for j in range(lo, hi)], 1)
        sums = jnp.dot(full, block, preferred_element_type=F32)
        for j in range(lo, hi):
            at = (j - lo) * half
            store_grads(sums[:, at : at + half] + offset, turned[j], grads, j)
    grads[ny] = jnp.zeros(grads.shape[1:], BF)
    copies.start(grads, grads_out)
    terms[...] = weight_terms(
        [
            (
                [plane[1 + 2 * j : 3 + 2 * j] for plane in planes[1:]],
                [grads[j, :cout], grads[j + 1, :cout]],
            )
            for j in range(ny)
        ]
    )
    copies.wait()


def halo_kernel(first, last, *refs):
    halo, lines, pre_in, turned_in, front, terms_in = refs[:6]
    refs = refs[6:]
    if not first:
        before, grads_in = refs[:2]
        refs = refs[2:]
    grads_out, raw_out = refs[:2]
    refs = refs[2:]
    if last:
        packed = refs[0]
        refs = refs[1:]
    else:
        terms_out, carry_out = refs[:2]
        refs = refs[2:]
    below, own, pre, turned, grads, raw, held, semaphores = refs
    half = below.shape[-1]
    cout = front.shape[0]
    count = raw.shape[0]
    ny = pre_in.shape[0]
    start = 0 if first else ny - count
    rows = 2 * count
    lead = 0 if first else 2
    copies = Copies(semaphores)
    early = [
        copies.start(pre_in.at[start : start + count], pre),
        copies.start(turned_in.at[start : start + count], turned),
    ]
    begin = 2 * start + 1 - lead
    late = [
        copies.start(lines.at[:, begin : 2 * start + 1 + rows], own.at[:, 0 : rows + lead])
    ]
    if first:
        below[0] = jnp.zeros(below.shape[1:], BF)
    else:
        late.append(copies.start(grads_in.at[start - 1], held.at[0]))
        below[0] = before[1]
    table = picks(half, False)
    split_plane(lambda y: halo[:, 0, pl.ds(y, 16), :], below, table)
    copies.wait(*early)
    for lo, hi in spans(count, 8):
        block = jnp.concatenate([window([below], j, 3) for j in range(lo, hi)], 1)
        sums = jnp.dot(front[...], block, preferred_element_type=F32)
        for j in range(lo, hi):
            at = (j - lo) * half
            store_grads(sums[:, at : at + half] + pre[j], turned[j].astype(F32), grads, j)
            raw[j] = grads[j, :cout, :]
    size = count
    if last:
        grads[count] = jnp.zeros(grads.shape[1:], BF)
        size += 1
    copies.start(raw, raw_out)
    copies.start(grads.at[0:size], grads_out.at[start : start + size])
    copies.wait(*late)
    cells = []
    if not first:
        cells.append(
            (
                [before[...], own[0, 0:2], own[1, 0:2]],
                [held[0, :cout], grads[0, :cout]],
            )
        )
    for j in range(count if last else count - 1):
        at = 2 * j + lead
        cells.append(
            (
                [below[2 * j + 1 : 2 * j + 3], own[0, at : at + 2], own[1, at : at + 2]],
                [grads[j, :cout], grads[j + 1, :cout]],
            )
        )
    terms = terms_in[...] + weight_terms(cells)
    if last:
        pack(terms, packed, below.shape[1], cout)
    else:
        terms_out[...] = terms
        carry_out[...] = below[rows - 1 : rows + 1]
    copies.wait()


def pack(terms, packed, count, cout):
    for a in range(3):
        packed[a * count : (a + 1) * count] = terms[(2 * a + 1) * count : (2 * a + 2) * count]
    middle = jnp.concatenate([terms[2 * a * count : (2 * a + 1) * count, :cout] for a in range(3)], 0)
    rows = middle.shape[0] // 2
    packed[3 * count : 3 * count + rows] = jnp.concatenate([middle[:rows], middle[rows:]], 1)
    packed[3 * count + rows :] = jnp.concatenate(
        [terms[6 * count :][:, :cout], jnp.zeros((16, cout), F32)], 1
    )


def finish_kernel(packed, weight_grad, bias_grad):
    count = weight_grad.shape[2]
    cout = weight_grad.shape[3]
    for a in range(3):
        block = packed[a * count : (a + 1) * count]
        weight_grad[a, 2] = block[:, :cout]
        weight_grad[a, 0] = block[:, cout:]
    rows = 3 * count // 2
    middle = packed[3 * count : 3 * count + rows]
    middle = jnp.concatenate([middle[:, :cout], middle[:, cout:]], 0)
    for a in range(3):
        weight_grad[a, 1] = middle[a * count : (a + 1) * count]
    bias_grad[...] = packed[3 * count + rows :][:1, :cout]


def back_kernel(z, odd, fresh, aliased, *refs):
    refs = refs[1:] if aliased else refs
    back, grads_in = refs[:2]
    above_in = refs[2 : 2 + (2 if fresh else odd)]
    refs = refs[2 + len(above_in) :]
    total, grads, above, plane, semaphores = refs[:5]
    ny = grads.shape[0] - 1
    cout = grads.shape[1] // 2
    copies = Copies(semaphores)
    loads = []
    for lo, hi in spans(ny, 8):
        top = ny + 1 if hi == ny else hi
        part = [copies.start(grads_in.at[lo:top], grads.at[lo:top])]
        if odd and not fresh:
            part.append(copies.start(above_in[0].at[lo:top], above.at[lo:top]))
        loads.append(part)
    if fresh:
        at = 0
        for ref in above_in:
            for j in range(ref.shape[0]):
                above[at + j, :cout, :] = ref[j]
                above[at + j, cout:, :] = earlier(ref[j].astype(F32)).astype(BF)
            at += ref.shape[0]
        above[ny] = jnp.zeros(above.shape[1:], BF)
    left = jnp.concatenate([back[2], back[0]], 1) if odd else back[1]
    cin = plane.shape[0]
    half = plane.shape[2] // 2
    table = picks(half, True)
    copies.wait(*loads[0])
    for n, (lo, hi) in enumerate(spans(ny, 8)):
        if n + 1 < len(loads):
            copies.wait(*loads[n + 1])
        columns = []
        for j in range(lo, hi):
            parts = [grads[j : j + 2].reshape(-1, half)]
            if odd:
                parts.append(above[j : j + 2].reshape(-1, half))
            columns.append(jnp.concatenate(parts, 0))
        sums = jnp.dot(left, jnp.concatenate(columns, 1), preferred_element_type=F32)
        sums = sums.astype(BF)
        rows = []
        for j in range(hi - lo):
            for py in range(2):
                lanes = slice(j * half, (j + 1) * half)
                even = sums[py * cin : (py + 1) * cin, lanes]
                odds = sums[(2 + py) * cin : (3 + py) * cin, lanes]
                rows.append(jnp.concatenate([even, odds], 1))
        merged = jnp.dot(jnp.concatenate(rows, 0), table, preferred_element_type=F32)
        merged = merged.astype(BF).reshape(2 * (hi - lo), cin, 2 * half)
        plane[:, 2 * lo : 2 * hi, :] = jnp.swapaxes(merged, 0, 1)
        copies.start(plane.at[:, 2 * lo : 2 * hi], total.at[:, z, 2 * lo : 2 * hi])
    copies.wait()


def back_plane(z, total, full, back, grads, above=()):
    cin, depth, height, width = full
    fresh = len(above) == 2
    args = [back, grads, *above]
    specs = [VMEM, ANY] + [VMEM if fresh else ANY] * len(above)
    aliased = total is not None
    if aliased:
        args = [total] + args
        specs = [ANY] + specs
    return pl.pallas_call(
        functools.partial(back_kernel, z, len(above) > 0, fresh, aliased),
        in_specs=specs,
        out_specs=ANY,
        out_shape=shape(*full),
        scratch_shapes=[
            pltpu.VMEM(grads.shape, BF),
            pltpu.VMEM(grads.shape if above else (16, 128), BF),
            pltpu.VMEM((cin, height, width), BF),
            pltpu.SemaphoreType.DMA((3 * (height // 16),)),
        ],
        input_output_aliases={0: 0} if aliased else {},
        compiler_params=PARAMS,
        cost_estimate=cost(3 * 10**9, 4 * 2**20),
    )(*args)


def all_sum(value, axis):
    peers = lax.axis_size(axis)
    if peers & (peers - 1):
        return lax.psum(value, axis)
    if peers == 1:
        return value
    swap = [(i, i ^ 1) for i in range(peers)]
    odd = lax.axis_index(axis) & 1
    rows = value.shape[0] // 2
    halves = value.reshape(2, rows, value.shape[1])
    mine = lax.dynamic_index_in_dim(halves, odd, 0, False)
    other = lax.dynamic_index_in_dim(halves, 1 - odd, 0, False)
    mine = mine + lax.ppermute(other, axis, swap)
    step = 2
    while step < peers:
        mine = mine + lax.ppermute(mine, axis, [(i, i ^ step) for i in range(peers)])
        step *= 2
    other = lax.ppermute(mine, axis, swap)
    low = jnp.where(odd == 0, mine, other)
    high = jnp.where(odd == 0, other, mine)
    return jnp.concatenate([low, high], 0)


def shifted(x, axis, by):
    peers = lax.axis_size(axis)
    pairs = [(i, i + by) for i in range(peers) if 0 <= i + by < peers]
    return lax.ppermute(x, axis, pairs)


def shards(volume, weights, bias, upstream):
    cin, depth, height, width = volume.shape
    cout = bias.shape[0]
    ny, half = height // 2, width // 2
    rows, count = height + 1, 3 * cin
    cut = (height // 16 + 1) // 2 * 16
    halos = [
        shifted(volume[:, depth - 1 :, :cut], "slab", 1),
        shifted(volume[:, depth - 1 :, cut:], "slab", 1),
    ]
    grads_shape = (ny + 1, 2 * cout, half)
    terms_shape = (6 * count + 16, 2 * cout)
    lines, pre, turned, upper, terms, back, front = pl.pallas_call(
        first_kernel,
        in_specs=[ANY, VMEM, VMEM, ANY],
        out_specs=[ANY] * 4 + [VMEM] * 3,
        out_shape=[
            shape(2, rows, count, half),
            shape(ny, cout, half, dtype=F32),
            shape(ny, cout, half),
            shape(*grads_shape),
            shape(*terms_shape, dtype=F32),
            shape(3, 4 * cin, 4 * cout),
            shape(cout, 3 * count),
        ],
        scratch_shapes=[
            pltpu.VMEM((4, cin, height, width), BF),
            pltpu.VMEM((4, rows, count, half), BF),
            pltpu.VMEM((2, cout, ny, half), BF),
            pltpu.VMEM((ny, cout, half), F32),
            pltpu.VMEM((ny, cout, half), BF),
            pltpu.VMEM((ny, cout, half), F32),
            pltpu.VMEM(grads_shape, BF),
            pltpu.VMEM((cout, 3, 3 * count), BF),
            pltpu.SemaphoreType.DMA((16,)),
        ],
        compiler_params=PARAMS,
        cost_estimate=cost(10 * 10**9, 20 * 2**20),
    )(volume, weights, bias.reshape(cout, 1), upstream)
    full = volume.shape

    def scratch(cells):
        return [
            pltpu.VMEM((2 * cells + 1, count, half), BF),
            pltpu.VMEM((2, 2 * cells + 2, count, half), BF),
            pltpu.VMEM((cells, cout, half), F32),
            pltpu.VMEM((cells, cout, half), BF),
            pltpu.VMEM((cells + 1, 2 * cout, half), BF),
            pltpu.VMEM((cells, cout, half), BF),
            pltpu.VMEM((1, 2 * cout, half), BF),
            pltpu.SemaphoreType.DMA((8,)),
        ]

    cells = cut // 2
    lower, raw, terms, carry = pl.pallas_call(
        functools.partial(halo_kernel, True, False),
        in_specs=[VMEM, ANY, ANY, ANY, VMEM, VMEM],
        out_specs=[ANY, ANY, VMEM, VMEM],
        out_shape=[
            shape(*grads_shape),
            shape(cells, cout, half),
            shape(*terms_shape, dtype=F32),
            shape(2, count, half),
        ],
        scratch_shapes=scratch(cells),
        compiler_params=PARAMS,
        cost_estimate=cost(3 * 10**9, 6 * 2**20),
    )(halos[0], lines, pre, turned, front, terms)
    above = [shifted(raw, "slab", -1)]
    total = back_plane(2, None, full, back, upper)
    total, late, lower = lax.optimization_barrier((total, halos[1], lower))
    cells = ny - cells
    lower, raw, packed = pl.pallas_call(
        functools.partial(halo_kernel, False, True),
        in_specs=[VMEM, ANY, ANY, ANY, VMEM, VMEM, VMEM, ANY],
        out_specs=[ANY, ANY, VMEM],
        out_shape=[
            shape(*grads_shape),
            shape(cells, cout, half),
            shape(9 * count // 2 + 16, 2 * cout, dtype=F32),
        ],
        scratch_shapes=scratch(cells),
        input_output_aliases={7: 0},
        compiler_params=PARAMS,
        cost_estimate=cost(2 * 10**9, 4 * 2**20),
    )(late, lines, pre, turned, front, terms, carry, lower)
    above.append(shifted(raw, "slab", -1))
    packed = all_sum(packed, "slab")
    total = back_plane(0, total, full, back, lower)
    total = back_plane(1, total, full, back, lower, (upper,))
    total = back_plane(3, total, full, back, upper, tuple(above))
    weight_grad, bias_grad = pl.pallas_call(
        finish_kernel,
        in_specs=[VMEM],
        out_specs=[VMEM] * 2,
        out_shape=[shape(3, 3, count, cout, dtype=F32), shape(1, cout, dtype=F32)],
        compiler_params=PARAMS,
    )(packed)
    return (
        total,
        weight_grad.reshape(3, 3, 3, cin, cout),
        bias_grad.reshape(cout),
    )


def solution(mesh):
    placed = (
        P(None, ("groups", "slab"), None, None),
        P(),
        P(),
        P(None, ("groups", "slab"), None, None),
    )
    return jax.shard_map(
        shards,
        mesh=mesh,
        in_specs=placed,
        out_specs=(
            P(None, ("groups", "slab"), None, None),
            P("groups", None, None, None, None),
            P("groups"),
        ),
        check_vma=False,
    )
```

```python
import functools

import jax
import jax.numpy as jnp
from jax import lax
from jax.experimental import pallas as pl
from jax.experimental.pallas import tpu as pltpu
from jax.sharding import PartitionSpec as P

BF = jnp.bfloat16
F32 = jnp.float32
VMEM = pl.BlockSpec(memory_space=pltpu.VMEM)
ANY = pl.BlockSpec(memory_space=pl.ANY)
HBM = pl.BlockSpec(memory_space=pltpu.HBM)
SMEM = pl.BlockSpec(memory_space=pltpu.SMEM)
PARAMS = pltpu.CompilerParams(vmem_limit_bytes=40 * 2**20)


def shape(*dims, dtype=BF):
    return jax.ShapeDtypeStruct(dims, dtype)


def cost(flops, size):
    return pl.CostEstimate(flops=flops, bytes_accessed=size, transcendentals=0)


def picks(half, inverse):
    if inverse:
        row = lax.broadcasted_iota(jnp.int32, (2 * half, 2 * half), 0)
        col = lax.broadcasted_iota(jnp.int32, (2 * half, 2 * half), 1)
        hit = jnp.where(row < half, 2 * row, 2 * (row - half) + 1) == col
    else:
        row = lax.broadcasted_iota(jnp.int32, (2 * half, 3 * half), 0)
        col = lax.broadcasted_iota(jnp.int32, (2 * half, 3 * half), 1)
        early = 2 * col - 1
        even = 2 * (col - half)
        odd = 2 * (col - 2 * half) + 1
        hit = jnp.where(col < half, early, jnp.where(col < 2 * half, even, odd)) == row
    return jnp.where(hit, 1.0, 0.0).astype(BF)


def split_plane(read, lines, table):
    rows, channels, half = lines.shape
    channels //= 3

    def step(t, carry):
        block = jnp.swapaxes(read(pl.multiple_of(t * 16, 16)), 0, 1)
        flat = block.reshape(16 * channels, 2 * half)
        taps = jnp.dot(flat, table, preferred_element_type=F32).astype(BF)
        taps = taps.reshape(16, channels, 3 * half)
        for e in range(3):
            lines[pl.ds(1 + t * 16, 16), e * channels : (e + 1) * channels, :] = taps[
                :, :, e * half : (e + 1) * half
            ]
        return carry

    lax.fori_loop(0, (rows - 1) // 16, step, 0, unroll=True)


def turn_upstream(upstream, turned):
    for o in range(0, upstream.shape[0], 8):
        block = upstream[o : o + 8].astype(F32)
        turned[:, o : o + 8, :] = jnp.swapaxes(block, 0, 1).astype(turned.dtype)


def earlier(values):
    cells = values.shape[-1]
    lane = lax.broadcasted_iota(jnp.int32, values.shape, values.ndim - 1)
    return jnp.where(lane == cells - 1, 0.0, pltpu.roll(values, cells - 1, values.ndim - 1))


def store_grads(pre, upstream, grads, j):
    slope = 0.6 + 0.4 * jnp.tanh(0.5 * pre)
    value = (upstream * slope).astype(BF)
    cout = value.shape[0]
    grads[j, :cout, :] = value
    grads[j, cout:, :] = earlier(value.astype(F32)).astype(BF)


def window(planes, j, count):
    parts = [plane[2 * j : 2 * j + count].reshape(-1, plane.shape[-1]) for plane in planes]
    return parts[0] if len(parts) == 1 else jnp.concatenate(parts, 0)


def weight_terms(cells):
    left, right = [], []
    for lines, grads in cells:
        flat = [line.reshape(-1, line.shape[-1]) for line in lines]
        ones = jnp.ones((16, flat[0].shape[-1]), BF)
        left.append(jnp.concatenate(flat + [ones], 0))
        right.append(jnp.concatenate(grads, 0))
    return lax.dot_general(
        jnp.concatenate(left, 1),
        jnp.concatenate(right, 1),
        (((1,), (1,)), ((), ())),
        preferred_element_type=F32,
    )


class Copies:
    def __init__(self, semaphores):
        self.semaphores, self.used, self.pending = semaphores, 0, []

    def start(self, source, target):
        copy = pltpu.make_async_copy(source, target, self.semaphores.at[self.used])
        self.used += 1
        copy.start()
        self.pending.append(copy)
        return copy

    def wait(self, *copies):
        for copy in copies or list(self.pending):
            copy.wait()
            self.pending.remove(copy)


def spans(total, size):
    return [(at, min(at + size, total)) for at in range(0, total, size)]


def column(bias):
    cout = bias.shape[1]
    row = lax.broadcasted_iota(jnp.int32, (cout, cout), 0)
    col = lax.broadcasted_iota(jnp.int32, (cout, cout), 1)
    return jnp.sum(jnp.where(row == col, bias[...], 0.0), axis=1, keepdims=True)


def lower_kernel(
    volume, weights_in, bias, upstream,
    lines, pre, late, full, back,
    field, inputs, weights, semaphores,
):
    cin = volume.shape[0]
    cout = bias.shape[1]
    half = volume.shape[3] // 2
    ny = upstream.shape[2]
    copies = Copies(semaphores)
    kernel = copies.start(weights_in, weights)
    ins = [copies.start(volume.at[:, z], field.at[z]) for z in range(2)]
    ups = copies.start(upstream.at[:, 0], inputs)
    table = picks(half, False)
    copies.wait(kernel)
    for a in range(3):
        for b in range(3):
            block = jnp.concatenate([weights[a, b, e] for e in range(3)], 0)
            at = (3 * a + b) * 3 * cin
            full[:, at : at + 3 * cin] = block.T
    blank = jnp.zeros((cin, cout), BF)
    for a in range(3):
        for px in range(2):
            for py in range(2):
                row = []
                for dy in range(2):
                    for dx in range(2):
                        b, e = py + 1 - 2 * dy, px + 1 - 2 * dx
                        row.append(weights[a, b, e] if b >= 0 and e >= 0 else blank)
                at = (px * 2 + py) * cin
                back[a, at : at + cin, :] = jnp.concatenate(row, 1)
    planes = [lines.at[z] for z in range(2)]
    for z in range(2):
        planes[z][0] = jnp.zeros(planes[z].shape[1:], BF)
        copies.wait(ins[z])
        split_plane(lambda y, z=z: field[z, :, pl.ds(y, 16), :], planes[z], table)
    copies.wait(ups)
    turn_upstream(inputs, late)
    taps = full[:, 9 * cin :]
    offset = column(bias)
    for lo, hi in spans(ny, 8):
        block = jnp.concatenate([window(planes, j, 3) for j in range(lo, hi)], 1)
        sums = jnp.dot(taps, block, preferred_element_type=F32)
        for j in range(lo, hi):
            pre[j] = sums[:, (j - lo) * half : (j - lo + 1) * half] + offset


def upper_kernel(
    volume, lines, full, bias, upstream,
    grads, terms,
    field, middle, top, inputs, turned, semaphores,
):
    cout = bias.shape[1]
    half = volume.shape[3] // 2
    ny = upstream.shape[2]
    copies = Copies(semaphores)
    ins = [copies.start(volume.at[:, 2 + z], field.at[z]) for z in range(2)]
    ups = copies.start(upstream.at[:, 1], inputs)
    table = picks(half, False)
    planes = [lines.at[1], middle, top]
    for z in range(2):
        planes[1 + z][0] = jnp.zeros(top.shape[1:], BF)
        copies.wait(ins[z])
        split_plane(lambda y, z=z: field[z, :, pl.ds(y, 16), :], planes[1 + z], table)
    copies.wait(ups)
    turn_upstream(inputs, turned)
    offset = column(bias)
    for lo, hi in spans(ny, 8):
        block = jnp.concatenate([window(planes, j, 3) for j in range(lo, hi)], 1)
        sums = jnp.dot(full[...], block, preferred_element_type=F32)
        for j in range(lo, hi):
            at = (j - lo) * half
            store_grads(sums[:, at : at + half] + offset, turned[j], grads, j)
    grads[ny] = jnp.zeros(grads.shape[1:], BF)
    terms[...] = plane_terms(planes, grads)


def plane_terms(planes, grads):
    cout = grads.shape[1] // 2
    return weight_terms(
        [
            (
                [plane[1 + 2 * j : 3 + 2 * j] for plane in planes],
                [grads[j, :cout], grads[j + 1, :cout]],
            )
            for j in range(grads.shape[0] - 1)
        ]
    )


def halo_kernel(halo, pre, upstream, full, grads, raw, below):
    half = below.shape[-1]
    cout, ny = full.shape[0], pre.shape[0]
    below[0] = jnp.zeros(below.shape[1:], BF)
    split_plane(lambda y: halo[:, 0, pl.ds(y, 16), :], below, picks(half, False))
    front = full[:, : full.shape[1] // 3]
    for lo, hi in spans(ny, 8):
        block = jnp.concatenate([window([below], j, 3) for j in range(lo, hi)], 1)
        sums = jnp.dot(front, block, preferred_element_type=F32)
        for j in range(lo, hi):
            at = (j - lo) * half
            store_grads(sums[:, at : at + half] + pre[j], upstream[j].astype(F32), grads, j)
            raw[j] = grads[j, :cout, :]
    grads[ny] = jnp.zeros(grads.shape[1:], BF)


def terms_kernel(below, lines, grads, terms_in, packed):
    terms = terms_in[...] + plane_terms([below, lines.at[0], lines.at[1]], grads)
    pack(terms, packed, below.shape[1], grads.shape[1] // 2)


def pack(terms, packed, count, cout):
    for a in range(3):
        packed[a * count : (a + 1) * count] = terms[(2 * a + 1) * count : (2 * a + 2) * count]
    middle = jnp.concatenate([terms[2 * a * count : (2 * a + 1) * count, :cout] for a in range(3)], 0)
    rows = middle.shape[0] // 2
    packed[3 * count : 3 * count + rows] = jnp.concatenate([middle[:rows], middle[rows:]], 1)
    packed[3 * count + rows :] = jnp.concatenate(
        [terms[6 * count :][:, :cout], jnp.zeros((16, cout), F32)], 1
    )


def finish_kernel(mine, got, weight_grad, bias_grad):
    packed = mine[...].astype(F32) + got[...].astype(F32)
    count = weight_grad.shape[2]
    cout = weight_grad.shape[3]
    for a in range(3):
        block = packed[a * count : (a + 1) * count]
        weight_grad[a, 2] = block[:, :cout]
        weight_grad[a, 0] = block[:, cout:]
    rows = 3 * count // 2
    middle = packed[3 * count : 3 * count + rows]
    middle = jnp.concatenate([middle[:, :cout], middle[:, cout:]], 0)
    for a in range(3):
        weight_grad[a, 1] = middle[a * count : (a + 1) * count]
    bias_grad[...] = packed[3 * count + rows :][:1, :cout]


def back_kernel(z, odd, fresh, aliased, *refs):
    refs = refs[1:] if aliased else refs
    back, grads_in = refs[:2]
    above_in = refs[2 : 2 + odd]
    refs = refs[2 + len(above_in) :]
    total, grads, above, plane, semaphores = refs[:5]
    ny = grads.shape[0] - 1
    cout = grads.shape[1] // 2
    copies = Copies(semaphores)
    loads = []
    for lo, hi in spans(ny, 8):
        top = ny + 1 if hi == ny else hi
        part = [copies.start(grads_in.at[lo:top], grads.at[lo:top])]
        if odd and not fresh:
            part.append(copies.start(above_in[0].at[lo:top], above.at[lo:top]))
        loads.append(part)
    if fresh:
        for j in range(ny):
            value = above_in[0][j]
            above[j, :cout, :] = value
            above[j, cout:, :] = earlier(value.astype(F32)).astype(BF)
        above[ny] = jnp.zeros(above.shape[1:], BF)
    left = jnp.concatenate([back[2], back[0]], 1) if odd else back[1]
    cin = plane.shape[0]
    half = plane.shape[2] // 2
    table = picks(half, True)
    copies.wait(*loads[0])
    for n, (lo, hi) in enumerate(spans(ny, 8)):
        if n + 1 < len(loads):
            copies.wait(*loads[n + 1])
        columns = []
        for j in range(lo, hi):
            parts = [grads[j : j + 2].reshape(-1, half)]
            if odd:
                parts.append(above[j : j + 2].reshape(-1, half))
            columns.append(jnp.concatenate(parts, 0))
        sums = jnp.dot(left, jnp.concatenate(columns, 1), preferred_element_type=F32)
        sums = sums.astype(BF)
        rows = []
        for j in range(hi - lo):
            for py in range(2):
                lanes = slice(j * half, (j + 1) * half)
                even = sums[py * cin : (py + 1) * cin, lanes]
                odds = sums[(2 + py) * cin : (3 + py) * cin, lanes]
                rows.append(jnp.concatenate([even, odds], 1))
        merged = jnp.dot(jnp.concatenate(rows, 0), table, preferred_element_type=F32)
        merged = merged.astype(BF).reshape(2 * (hi - lo), cin, 2 * half)
        plane[:, 2 * lo : 2 * hi, :] = jnp.swapaxes(merged, 0, 1)
        copies.start(plane.at[:, 2 * lo : 2 * hi], total.at[:, z, 2 * lo : 2 * hi])
    copies.wait()


def back_plane(z, total, full, back, grads, above=()):
    cin, depth, height, width = full
    fresh = len(above) > 0 and above[0].shape != grads.shape
    args = [back, grads, *above]
    specs = [VMEM, ANY] + [VMEM if fresh else ANY] * len(above)
    aliased = total is not None
    if aliased:
        args = [total] + args
        specs = [ANY] + specs
    return pl.pallas_call(
        functools.partial(back_kernel, z, len(above) > 0, fresh, aliased),
        in_specs=specs,
        out_specs=ANY,
        out_shape=shape(*full),
        scratch_shapes=[
            pltpu.VMEM(grads.shape, BF),
            pltpu.VMEM(grads.shape if above else (16, 128), BF),
            pltpu.VMEM((cin, height, width), BF),
            pltpu.SemaphoreType.DMA((3 * (height // 16),)),
        ],
        input_output_aliases={0: 0} if aliased else {},
        compiler_params=PARAMS,
        cost_estimate=cost(3 * 10**9, 4 * 2**20),
    )(*args)


def all_sum(value, axis, total, above, works):
    peers = lax.axis_size(axis)
    works = list(works)
    got = lax.ppermute(value, axis, [(i, i ^ 1) for i in range(peers)])
    step = 2
    while step < peers:
        sent, total = lax.optimization_barrier(
            ((value.astype(F32) + got.astype(F32)).astype(BF), total)
        )
        value = sent
        got = lax.ppermute(sent, axis, [(i, i ^ step) for i in range(peers)])
        if works:
            total, above = works.pop(0)(total, above)
        got, total = lax.optimization_barrier((got, total))
        step *= 2
    for work in works:
        total, above = work(total, above)
    return value, got, total


def shifted(x, axis, by):
    peers = lax.axis_size(axis)
    pairs = [(i, i + by) for i in range(peers) if 0 <= i + by < peers]
    return lax.ppermute(x, axis, pairs)


def shards(volume, weights, bias, upstream):
    cin, depth, height, width = volume.shape
    cout = bias.shape[0]
    ny, half = height // 2, width // 2
    rows, count = height + 1, 3 * cin
    halo = shifted(volume[:, depth - 1 :], "slab", 1)
    grads_shape = (ny + 1, 2 * cout, half)
    terms_shape = (6 * count + 16, 2 * cout)
    bias = bias.reshape(1, cout)
    pinned = pltpu.with_memory_space_constraint(volume, pltpu.HBM)
    lines, pre, late, taps, back = pl.pallas_call(
        lower_kernel,
        in_specs=[ANY, ANY, VMEM, ANY],
        out_specs=[VMEM] * 5,
        out_shape=[
            shape(2, rows, count, half),
            shape(ny, cout, half, dtype=F32),
            shape(ny, cout, half),
            shape(cout, 9 * count),
            shape(3, 4 * cin, 4 * cout),
        ],
        scratch_shapes=[
            pltpu.VMEM((2, cin, height, width), BF),
            pltpu.VMEM((cout, ny, half), BF),
            pltpu.VMEM(weights.shape, BF),
            pltpu.SemaphoreType.DMA((4,)),
        ],
        compiler_params=PARAMS,
        cost_estimate=cost(5 * 10**9, 10 * 2**20),
    )(pinned, weights, bias, upstream)
    upper, terms = pl.pallas_call(
        upper_kernel,
        in_specs=[ANY, VMEM, VMEM, VMEM, ANY],
        out_specs=[VMEM] * 2,
        out_shape=[shape(*grads_shape), shape(*terms_shape, dtype=F32)],
        scratch_shapes=[
            pltpu.VMEM((2, cin, height, width), BF),
            pltpu.VMEM((rows, count, half), BF),
            pltpu.VMEM((rows, count, half), BF),
            pltpu.VMEM((cout, ny, half), BF),
            pltpu.VMEM((ny, cout, half), F32),
            pltpu.SemaphoreType.DMA((3,)),
        ],
        compiler_params=PARAMS,
        cost_estimate=cost(6 * 10**9, 10 * 2**20),
    )(pinned, lines, taps, bias, upstream)
    full = volume.shape

    total = back_plane(2, None, full, back, upper)
    total, halo = lax.optimization_barrier((total, halo))
    lower, raw, below = pl.pallas_call(
        halo_kernel,
        in_specs=[VMEM] * 4,
        out_specs=[VMEM] * 3,
        out_shape=[shape(*grads_shape), shape(ny, cout, half), shape(rows, count, half)],
        compiler_params=PARAMS,
        cost_estimate=cost(3 * 10**9, 6 * 2**20),
    )(halo, pre, late, taps)
    above = shifted(raw, "slab", -1)
    packed = pl.pallas_call(
        terms_kernel,
        in_specs=[VMEM] * 4,
        out_specs=VMEM,
        out_shape=shape(9 * count // 2 + 16, 2 * cout, dtype=F32),
        compiler_params=PARAMS,
        cost_estimate=cost(10**8, 10**5),
    )(below, lines, lower, terms)

    def middle(total, above):
        total, above = lax.optimization_barrier((total, above))
        return back_plane(1, total, full, back, lower, (upper,)), above

    packed, got, total = all_sum(
        packed,
        "slab",
        total,
        above,
        [
            lambda t, g: (back_plane(0, t, full, back, lower), g),
            middle,
            lambda t, g: (back_plane(3, t, full, back, upper, (g,)), g),
        ],
    )
    weight_grad, bias_grad = pl.pallas_call(
        finish_kernel,
        in_specs=[VMEM] * 2,
        out_specs=[VMEM] * 2,
        out_shape=[shape(3, 3, count, cout, dtype=F32), shape(1, cout, dtype=F32)],
        compiler_params=PARAMS,
    )(packed, got)
    return (
        total,
        weight_grad.reshape(3, 3, 3, cin, cout),
        bias_grad.reshape(cout),
    )


def solution(mesh):
    placed = (
        P(None, ("groups", "slab"), None, None),
        P(),
        P(),
        P(None, ("groups", "slab"), None, None),
    )
    return jax.shard_map(
        shards,
        mesh=mesh,
        in_specs=placed,
        out_specs=(
            P(None, ("groups", "slab"), None, None),
            P("groups", None, None, None, None),
            P("groups"),
        ),
        check_vma=False,
    )
```

```python
import functools

import jax
import jax.numpy as jnp
from jax import lax
from jax.experimental import pallas as pl
from jax.experimental.pallas import tpu as pltpu
from jax.sharding import PartitionSpec as P

BF = jnp.bfloat16
F32 = jnp.float32
VMEM = pl.BlockSpec(memory_space=pltpu.VMEM)
ANY = pl.BlockSpec(memory_space=pl.ANY)
HBM = pl.BlockSpec(memory_space=pltpu.HBM)
SMEM = pl.BlockSpec(memory_space=pltpu.SMEM)
PARAMS = pltpu.CompilerParams(vmem_limit_bytes=40 * 2**20)


def shape(*dims, dtype=BF):
    return jax.ShapeDtypeStruct(dims, dtype)


def cost(flops, size):
    return pl.CostEstimate(flops=flops, bytes_accessed=size, transcendentals=0)


def picks(half, inverse):
    if inverse:
        row = lax.broadcasted_iota(jnp.int32, (2 * half, 2 * half), 0)
        col = lax.broadcasted_iota(jnp.int32, (2 * half, 2 * half), 1)
        hit = jnp.where(row < half, 2 * row, 2 * (row - half) + 1) == col
    else:
        row = lax.broadcasted_iota(jnp.int32, (2 * half, 3 * half), 0)
        col = lax.broadcasted_iota(jnp.int32, (2 * half, 3 * half), 1)
        early = 2 * col - 1
        even = 2 * (col - half)
        odd = 2 * (col - 2 * half) + 1
        hit = jnp.where(col < half, early, jnp.where(col < 2 * half, even, odd)) == row
    return jnp.where(hit, 1.0, 0.0).astype(BF)


def split_plane(read, lines, table):
    rows, channels, half = lines.shape
    channels //= 3

    def step(t, carry):
        block = jnp.swapaxes(read(pl.multiple_of(t * 16, 16)), 0, 1)
        flat = block.reshape(16 * channels, 2 * half)
        taps = jnp.dot(flat, table, preferred_element_type=F32).astype(BF)
        taps = taps.reshape(16, channels, 3 * half)
        for e in range(3):
            lines[pl.ds(1 + t * 16, 16), e * channels : (e + 1) * channels, :] = taps[
                :, :, e * half : (e + 1) * half
            ]
        return carry

    lax.fori_loop(0, (rows - 1) // 16, step, 0, unroll=True)


def turn_upstream(upstream, turned):
    for o in range(0, upstream.shape[0], 8):
        block = upstream[o : o + 8].astype(F32)
        turned[:, o : o + 8, :] = jnp.swapaxes(block, 0, 1).astype(turned.dtype)


def earlier(values):
    cells = values.shape[-1]
    lane = lax.broadcasted_iota(jnp.int32, values.shape, values.ndim - 1)
    return jnp.where(lane == cells - 1, 0.0, pltpu.roll(values, cells - 1, values.ndim - 1))


def store_grads(pre, upstream, grads, j):
    slope = 0.6 + 0.4 * jnp.tanh(0.5 * pre)
    value = (upstream * slope).astype(BF)
    cout = value.shape[0]
    grads[j, :cout, :] = value
    grads[j, cout:, :] = earlier(value.astype(F32)).astype(BF)


def window(planes, j, count):
    parts = [plane[2 * j : 2 * j + count].reshape(-1, plane.shape[-1]) for plane in planes]
    return parts[0] if len(parts) == 1 else jnp.concatenate(parts, 0)


def weight_terms(cells):
    left, right = [], []
    for lines, grads in cells:
        flat = [line.reshape(-1, line.shape[-1]) for line in lines]
        ones = jnp.ones((16, flat[0].shape[-1]), BF)
        left.append(jnp.concatenate(flat + [ones], 0))
        right.append(jnp.concatenate(grads, 0))
    return lax.dot_general(
        jnp.concatenate(left, 1),
        jnp.concatenate(right, 1),
        (((1,), (1,)), ((), ())),
        preferred_element_type=F32,
    )


class Copies:
    def __init__(self, semaphores):
        self.semaphores, self.used, self.pending = semaphores, 0, []

    def start(self, source, target):
        copy = pltpu.make_async_copy(source, target, self.semaphores.at[self.used])
        self.used += 1
        copy.start()
        self.pending.append(copy)
        return copy

    def wait(self, *copies):
        for copy in copies or list(self.pending):
            copy.wait()
            self.pending.remove(copy)


def spans(total, size):
    return [(at, min(at + size, total)) for at in range(0, total, size)]


def column(bias):
    cout = bias.shape[1]
    row = lax.broadcasted_iota(jnp.int32, (cout, cout), 0)
    col = lax.broadcasted_iota(jnp.int32, (cout, cout), 1)
    return jnp.sum(jnp.where(row == col, bias[...], 0.0), axis=1, keepdims=True)


def lower_kernel(
    volume, weights_in, bias, upstream,
    lines, pre, late, full, back,
    field, inputs, weights, semaphores,
):
    cin = volume.shape[0]
    cout = bias.shape[1]
    half = volume.shape[3] // 2
    ny = upstream.shape[2]
    copies = Copies(semaphores)
    kernel = copies.start(weights_in, weights)
    ins = [copies.start(volume.at[:, z], field.at[z]) for z in range(2)]
    ups = copies.start(upstream.at[:, 0], inputs)
    table = picks(half, False)
    copies.wait(kernel)
    for a in range(3):
        for b in range(3):
            block = jnp.concatenate([weights[a, b, e] for e in range(3)], 0)
            at = (3 * a + b) * 3 * cin
            full[:, at : at + 3 * cin] = block.T
    blank = jnp.zeros((cin, cout), BF)
    for a in range(3):
        for px in range(2):
            for py in range(2):
                row = []
                for dy in range(2):
                    for dx in range(2):
                        b, e = py + 1 - 2 * dy, px + 1 - 2 * dx
                        row.append(weights[a, b, e] if b >= 0 and e >= 0 else blank)
                at = (px * 2 + py) * cin
                back[a, at : at + cin, :] = jnp.concatenate(row, 1)
    planes = [lines.at[z] for z in range(2)]
    for z in range(2):
        planes[z][0] = jnp.zeros(planes[z].shape[1:], BF)
        copies.wait(ins[z])
        split_plane(lambda y, z=z: field[z, :, pl.ds(y, 16), :], planes[z], table)
    copies.wait(ups)
    turn_upstream(inputs, late)
    taps = full[:, 9 * cin :]
    offset = column(bias)
    for lo, hi in spans(ny, 8):
        block = jnp.concatenate([window(planes, j, 3) for j in range(lo, hi)], 1)
        sums = jnp.dot(taps, block, preferred_element_type=F32)
        for j in range(lo, hi):
            pre[j] = sums[:, (j - lo) * half : (j - lo + 1) * half] + offset


def upper_kernel(
    volume, lines, full, bias, upstream,
    grads, terms,
    field, middle, top, inputs, turned, semaphores,
):
    cout = bias.shape[1]
    half = volume.shape[3] // 2
    ny = upstream.shape[2]
    copies = Copies(semaphores)
    ins = [copies.start(volume.at[:, 2 + z], field.at[z]) for z in range(2)]
    ups = copies.start(upstream.at[:, 1], inputs)
    table = picks(half, False)
    planes = [lines.at[1], middle, top]
    for z in range(2):
        planes[1 + z][0] = jnp.zeros(top.shape[1:], BF)
        copies.wait(ins[z])
        split_plane(lambda y, z=z: field[z, :, pl.ds(y, 16), :], planes[1 + z], table)
    copies.wait(ups)
    turn_upstream(inputs, turned)
    offset = column(bias)
    for lo, hi in spans(ny, 8):
        block = jnp.concatenate([window(planes, j, 3) for j in range(lo, hi)], 1)
        sums = jnp.dot(full[...], block, preferred_element_type=F32)
        for j in range(lo, hi):
            at = (j - lo) * half
            store_grads(sums[:, at : at + half] + offset, turned[j], grads, j)
    grads[ny] = jnp.zeros(grads.shape[1:], BF)
    terms[...] = plane_terms(planes, grads)


def plane_terms(planes, grads):
    cout = grads.shape[1] // 2
    return weight_terms(
        [
            (
                [plane[1 + 2 * j : 3 + 2 * j] for plane in planes],
                [grads[j, :cout], grads[j + 1, :cout]],
            )
            for j in range(grads.shape[0] - 1)
        ]
    )


def halo_kernel(halo, pre, upstream, full, grads, raw, below):
    half = below.shape[-1]
    cout, ny = full.shape[0], pre.shape[0]
    below[0] = jnp.zeros(below.shape[1:], BF)
    split_plane(lambda y: halo[:, 0, pl.ds(y, 16), :], below, picks(half, False))
    front = full[:, : full.shape[1] // 3]
    for lo, hi in spans(ny, 8):
        block = jnp.concatenate([window([below], j, 3) for j in range(lo, hi)], 1)
        sums = jnp.dot(front, block, preferred_element_type=F32)
        for j in range(lo, hi):
            at = (j - lo) * half
            store_grads(sums[:, at : at + half] + pre[j], upstream[j].astype(F32), grads, j)
            raw[j] = grads[j, :cout, :]
    grads[ny] = jnp.zeros(grads.shape[1:], BF)


def terms_kernel(below, lines, grads, terms_in, packed):
    terms = terms_in[...] + plane_terms([below, lines.at[0], lines.at[1]], grads)
    pack(terms, packed, below.shape[1], grads.shape[1] // 2, lax.axis_index("slab"))


def pack(terms, packed, count, cout, place):
    for a in range(3):
        packed[a * count : (a + 1) * count] = terms[(2 * a + 1) * count : (2 * a + 2) * count]
    middle = jnp.concatenate([terms[2 * a * count : (2 * a + 1) * count, :cout] for a in range(3)], 0)
    rows = middle.shape[0] // 2
    packed[3 * count : 3 * count + rows] = jnp.concatenate([middle[:rows], middle[rows:]], 1)
    total = terms[6 * count : 6 * count + 8, :cout]
    high = total.astype(BF).astype(F32)
    both = jnp.concatenate([high, total - high], 1)
    slots = packed.shape[0] - 3 * count - rows
    row = lax.broadcasted_iota(jnp.int32, (slots, 2 * cout), 0)
    packed[3 * count + rows :] = jnp.where(
        row == place, jnp.broadcast_to(both[:1], (slots, 2 * cout)), 0.0
    )


def finish_kernel(mine, got, weight_grad, bias_grad):
    packed = mine[...].astype(F32) + got[...].astype(F32)
    count = weight_grad.shape[2]
    cout = weight_grad.shape[3]
    for a in range(3):
        block = packed[a * count : (a + 1) * count]
        weight_grad[a, 2] = block[:, :cout]
        weight_grad[a, 0] = block[:, cout:]
    rows = 3 * count // 2
    middle = packed[3 * count : 3 * count + rows]
    middle = jnp.concatenate([middle[:, :cout], middle[:, cout:]], 0)
    for a in range(3):
        weight_grad[a, 1] = middle[a * count : (a + 1) * count]
    total = jnp.sum(packed[3 * count + rows :], axis=0, keepdims=True)
    bias_grad[...] = total[:, :cout] + total[:, cout:]


def back_kernel(z, odd, fresh, aliased, *refs):
    refs = refs[1:] if aliased else refs
    back, grads_in = refs[:2]
    above_in = refs[2 : 2 + odd]
    refs = refs[2 + len(above_in) :]
    total, grads, above, plane, semaphores = refs[:5]
    ny = grads.shape[0] - 1
    cout = grads.shape[1] // 2
    copies = Copies(semaphores)
    loads = []
    for lo, hi in spans(ny, 8):
        top = ny + 1 if hi == ny else hi
        part = [copies.start(grads_in.at[lo:top], grads.at[lo:top])]
        if odd and not fresh:
            part.append(copies.start(above_in[0].at[lo:top], above.at[lo:top]))
        loads.append(part)
    if fresh:
        for j in range(ny):
            value = above_in[0][j]
            above[j, :cout, :] = value
            above[j, cout:, :] = earlier(value.astype(F32)).astype(BF)
        above[ny] = jnp.zeros(above.shape[1:], BF)
    left = jnp.concatenate([back[2], back[0]], 1) if odd else back[1]
    cin = plane.shape[0]
    half = plane.shape[2] // 2
    table = picks(half, True)
    copies.wait(*loads[0])
    for n, (lo, hi) in enumerate(spans(ny, 8)):
        if n + 1 < len(loads):
            copies.wait(*loads[n + 1])
        columns = []
        for j in range(lo, hi):
            parts = [grads[j : j + 2].reshape(-1, half)]
            if odd:
                parts.append(above[j : j + 2].reshape(-1, half))
            columns.append(jnp.concatenate(parts, 0))
        sums = jnp.dot(left, jnp.concatenate(columns, 1), preferred_element_type=F32)
        sums = sums.astype(BF)
        rows = []
        for j in range(hi - lo):
            for py in range(2):
                lanes = slice(j * half, (j + 1) * half)
                even = sums[py * cin : (py + 1) * cin, lanes]
                odds = sums[(2 + py) * cin : (3 + py) * cin, lanes]
                rows.append(jnp.concatenate([even, odds], 1))
        merged = jnp.dot(jnp.concatenate(rows, 0), table, preferred_element_type=F32)
        merged = merged.astype(BF).reshape(2 * (hi - lo), cin, 2 * half)
        plane[:, 2 * lo : 2 * hi, :] = jnp.swapaxes(merged, 0, 1)
        copies.start(plane.at[:, 2 * lo : 2 * hi], total.at[:, z, 2 * lo : 2 * hi])
    copies.wait()


def back_plane(z, total, full, back, grads, above=()):
    cin, depth, height, width = full
    fresh = len(above) > 0 and above[0].shape != grads.shape
    args = [back, grads, *above]
    specs = [VMEM, ANY] + [VMEM if fresh else ANY] * len(above)
    aliased = total is not None
    if aliased:
        args = [total] + args
        specs = [ANY] + specs
    return pl.pallas_call(
        functools.partial(back_kernel, z, len(above) > 0, fresh, aliased),
        in_specs=specs,
        out_specs=ANY,
        out_shape=shape(*full),
        scratch_shapes=[
            pltpu.VMEM(grads.shape, BF),
            pltpu.VMEM(grads.shape if above else (16, 128), BF),
            pltpu.VMEM((cin, height, width), BF),
            pltpu.SemaphoreType.DMA((3 * (height // 16),)),
        ],
        input_output_aliases={0: 0} if aliased else {},
        compiler_params=PARAMS,
        cost_estimate=cost(10**6, 10**3),
    )(*args)


def all_sum(value, axis, total, above, works):
    peers = lax.axis_size(axis)
    works = list(works)
    value, total = lax.optimization_barrier((value, total))
    got = lax.ppermute(value, axis, [(i, i ^ 1) for i in range(peers)])
    total, above = works.pop(0)(total, above)
    got, total = lax.optimization_barrier((got, total))
    step = 2
    while step < peers:
        sent, total = lax.optimization_barrier(
            ((value.astype(F32) + got.astype(F32)).astype(BF), total)
        )
        value = sent
        got = lax.ppermute(sent, axis, [(i, i ^ step) for i in range(peers)])
        if works:
            total, above = works.pop(0)(total, above)
        got, total, above = lax.optimization_barrier((got, total, above))
        step *= 2
    for work in works:
        total, above = work(total, above)
    return value, got, total


def shifted(x, axis, by):
    peers = lax.axis_size(axis)
    pairs = [(i, i + by) for i in range(peers) if 0 <= i + by < peers]
    return lax.ppermute(x, axis, pairs)


def shards(volume, weights, bias, upstream):
    cin, depth, height, width = volume.shape
    cout = bias.shape[0]
    ny, half = height // 2, width // 2
    rows, count = height + 1, 3 * cin
    halo = shifted(volume[:, depth - 1 :], "slab", 1)
    grads_shape = (ny + 1, 2 * cout, half)
    terms_shape = (6 * count + 16, 2 * cout)
    bias = bias.reshape(1, cout)
    pinned = pltpu.with_memory_space_constraint(volume, pltpu.HBM)
    lines, pre, late, taps, back = pl.pallas_call(
        lower_kernel,
        in_specs=[ANY, ANY, VMEM, ANY],
        out_specs=[VMEM] * 5,
        out_shape=[
            shape(2, rows, count, half),
            shape(ny, cout, half, dtype=F32),
            shape(ny, cout, half),
            shape(cout, 9 * count),
            shape(3, 4 * cin, 4 * cout),
        ],
        scratch_shapes=[
            pltpu.VMEM((2, cin, height, width), BF),
            pltpu.VMEM((cout, ny, half), BF),
            pltpu.VMEM(weights.shape, BF),
            pltpu.SemaphoreType.DMA((4,)),
        ],
        compiler_params=PARAMS,
        cost_estimate=cost(5 * 10**9, 10 * 2**20),
    )(pinned, weights, bias, upstream)
    upper, terms = pl.pallas_call(
        upper_kernel,
        in_specs=[ANY, VMEM, VMEM, VMEM, ANY],
        out_specs=[VMEM] * 2,
        out_shape=[shape(*grads_shape), shape(*terms_shape, dtype=F32)],
        scratch_shapes=[
            pltpu.VMEM((2, cin, height, width), BF),
            pltpu.VMEM((rows, count, half), BF),
            pltpu.VMEM((rows, count, half), BF),
            pltpu.VMEM((cout, ny, half), BF),
            pltpu.VMEM((ny, cout, half), F32),
            pltpu.SemaphoreType.DMA((3,)),
        ],
        compiler_params=PARAMS,
        cost_estimate=cost(6 * 10**9, 10 * 2**20),
    )(pinned, lines, taps, bias, upstream)
    full = volume.shape

    total = back_plane(2, None, full, back, upper)
    total, halo = lax.optimization_barrier((total, halo))
    lower, raw, below = pl.pallas_call(
        halo_kernel,
        in_specs=[VMEM] * 4,
        out_specs=[VMEM] * 3,
        out_shape=[shape(*grads_shape), shape(ny, cout, half), shape(rows, count, half)],
        compiler_params=PARAMS,
        cost_estimate=cost(3 * 10**9, 6 * 2**20),
    )(halo, pre, late, taps)
    slots = (lax.axis_size("slab") + 15) // 16 * 16
    above = shifted(raw, "slab", -1)
    packed = pl.pallas_call(
        terms_kernel,
        in_specs=[VMEM] * 4,
        out_specs=VMEM,
        out_shape=shape(9 * count // 2 + slots, 2 * cout, dtype=F32),
        compiler_params=PARAMS,
        cost_estimate=cost(10**8, 10**5),
    )(below, lines, lower, terms)

    packed, got, total = all_sum(
        packed,
        "slab",
        total,
        above,
        [
            lambda t, g: (back_plane(0, t, full, back, lower), g),
            lambda t, g: (back_plane(1, t, full, back, lower, (upper,)), g),
            lambda t, g: (back_plane(3, t, full, back, upper, (g,)), g),
        ],
    )
    weight_grad, bias_grad = pl.pallas_call(
        finish_kernel,
        in_specs=[VMEM] * 2,
        out_specs=[VMEM] * 2,
        out_shape=[shape(3, 3, count, cout, dtype=F32), shape(1, cout, dtype=F32)],
        compiler_params=PARAMS,
    )(packed, got)
    return (
        total,
        weight_grad.reshape(3, 3, 3, cin, cout),
        bias_grad.reshape(cout),
    )


def solution(mesh):
    placed = (
        P(None, ("groups", "slab"), None, None),
        P(),
        P(),
        P(None, ("groups", "slab"), None, None),
    )
    return jax.shard_map(
        shards,
        mesh=mesh,
        in_specs=placed,
        out_specs=(
            P(None, ("groups", "slab"), None, None),
            P("groups", None, None, None, None),
            P("groups"),
        ),
        check_vma=False,
    )
```

```python
import functools

import jax
import jax.numpy as jnp
from jax import lax
from jax.experimental import pallas as pl
from jax.experimental.pallas import tpu as pltpu
from jax.sharding import PartitionSpec as P

BF = jnp.bfloat16
F32 = jnp.float32
VMEM = pl.BlockSpec(memory_space=pltpu.VMEM)
ANY = pl.BlockSpec(memory_space=pl.ANY)
HBM = pl.BlockSpec(memory_space=pltpu.HBM)
SMEM = pl.BlockSpec(memory_space=pltpu.SMEM)
PARAMS = pltpu.CompilerParams(vmem_limit_bytes=40 * 2**20)


def shape(*dims, dtype=BF):
    return jax.ShapeDtypeStruct(dims, dtype)


def cost(flops, size):
    return pl.CostEstimate(flops=flops, bytes_accessed=size, transcendentals=0)


def picks(half, inverse):
    if inverse:
        row = lax.broadcasted_iota(jnp.int32, (2 * half, 2 * half), 0)
        col = lax.broadcasted_iota(jnp.int32, (2 * half, 2 * half), 1)
        hit = jnp.where(row < half, 2 * row, 2 * (row - half) + 1) == col
    else:
        row = lax.broadcasted_iota(jnp.int32, (2 * half, 3 * half), 0)
        col = lax.broadcasted_iota(jnp.int32, (2 * half, 3 * half), 1)
        early = 2 * col - 1
        even = 2 * (col - half)
        odd = 2 * (col - 2 * half) + 1
        hit = jnp.where(col < half, early, jnp.where(col < 2 * half, even, odd)) == row
    return jnp.where(hit, 1.0, 0.0).astype(BF)


def split_plane(read, lines, table):
    rows, channels, half = lines.shape
    channels //= 3

    def step(t, carry):
        block = jnp.swapaxes(read(pl.multiple_of(t * 16, 16)), 0, 1)
        flat = block.reshape(16 * channels, 2 * half)
        taps = jnp.dot(flat, table, preferred_element_type=F32).astype(BF)
        taps = taps.reshape(16, channels, 3 * half)
        for e in range(3):
            lines[pl.ds(1 + t * 16, 16), e * channels : (e + 1) * channels, :] = taps[
                :, :, e * half : (e + 1) * half
            ]
        return carry

    lax.fori_loop(0, (rows - 1) // 16, step, 0, unroll=True)


def turn_upstream(upstream, turned):
    for o in range(0, upstream.shape[0], 8):
        block = upstream[o : o + 8].astype(F32)
        turned[:, o : o + 8, :] = jnp.swapaxes(block, 0, 1).astype(turned.dtype)


def earlier(values):
    cells = values.shape[-1]
    lane = lax.broadcasted_iota(jnp.int32, values.shape, values.ndim - 1)
    return jnp.where(lane == cells - 1, 0.0, pltpu.roll(values, cells - 1, values.ndim - 1))


def store_grads(pre, upstream, grads, j):
    slope = 0.6 + 0.4 * jnp.tanh(0.5 * pre)
    value = (upstream * slope).astype(BF)
    cout = value.shape[0]
    grads[j, :cout, :] = value
    grads[j, cout:, :] = earlier(value.astype(F32)).astype(BF)


def window(planes, j, count):
    parts = [plane[2 * j : 2 * j + count].reshape(-1, plane.shape[-1]) for plane in planes]
    return parts[0] if len(parts) == 1 else jnp.concatenate(parts, 0)


def weight_terms(cells):
    left, right = [], []
    for lines, grads in cells:
        flat = [line.reshape(-1, line.shape[-1]) for line in lines]
        ones = jnp.ones((16, flat[0].shape[-1]), BF)
        left.append(jnp.concatenate(flat + [ones], 0))
        right.append(jnp.concatenate(grads, 0))
    return lax.dot_general(
        jnp.concatenate(left, 1),
        jnp.concatenate(right, 1),
        (((1,), (1,)), ((), ())),
        preferred_element_type=F32,
    )


class Copies:
    def __init__(self, semaphores):
        self.semaphores, self.used, self.pending = semaphores, 0, []

    def start(self, source, target):
        copy = pltpu.make_async_copy(source, target, self.semaphores.at[self.used])
        self.used += 1
        copy.start()
        self.pending.append(copy)
        return copy

    def wait(self, *copies):
        for copy in copies or list(self.pending):
            copy.wait()
            self.pending.remove(copy)


def spans(total, size):
    return [(at, min(at + size, total)) for at in range(0, total, size)]


def column(bias):
    cout = bias.shape[1]
    row = lax.broadcasted_iota(jnp.int32, (cout, cout), 0)
    col = lax.broadcasted_iota(jnp.int32, (cout, cout), 1)
    return jnp.sum(jnp.where(row == col, bias[...], 0.0), axis=1, keepdims=True)


def lower_kernel(
    volume, weights_in, bias, upstream,
    lines, pre, late, full, back,
    field, inputs, weights, semaphores,
):
    cin = volume.shape[0]
    cout = bias.shape[1]
    half = volume.shape[3] // 2
    ny = upstream.shape[2]
    copies = Copies(semaphores)
    kernel = copies.start(weights_in, weights)
    ins = [copies.start(volume.at[:, z], field.at[z]) for z in range(2)]
    ups = copies.start(upstream.at[:, 0], inputs)
    table = picks(half, False)
    copies.wait(kernel)
    for a in range(3):
        for b in range(3):
            block = jnp.concatenate([weights[a, b, e] for e in range(3)], 0)
            at = (3 * a + b) * 3 * cin
            full[:, at : at + 3 * cin] = block.T
    blank = jnp.zeros((cin, cout), BF)
    for a in range(3):
        for px in range(2):
            for py in range(2):
                row = []
                for dy in range(2):
                    for dx in range(2):
                        b, e = py + 1 - 2 * dy, px + 1 - 2 * dx
                        row.append(weights[a, b, e] if b >= 0 and e >= 0 else blank)
                at = (px * 2 + py) * cin
                back[a, at : at + cin, :] = jnp.concatenate(row, 1)
    planes = [lines.at[z] for z in range(2)]
    for z in range(2):
        planes[z][0] = jnp.zeros(planes[z].shape[1:], BF)
        copies.wait(ins[z])
        split_plane(lambda y, z=z: field[z, :, pl.ds(y, 16), :], planes[z], table)
    copies.wait(ups)
    turn_upstream(inputs, late)
    taps = full[:, 9 * cin :]
    offset = column(bias)
    for lo, hi in spans(ny, 8):
        block = jnp.concatenate([window(planes, j, 3) for j in range(lo, hi)], 1)
        sums = jnp.dot(taps, block, preferred_element_type=F32)
        for j in range(lo, hi):
            pre[j] = sums[:, (j - lo) * half : (j - lo + 1) * half] + offset


def upper_kernel(
    volume, lines, full, bias, upstream,
    grads, terms,
    field, middle, top, inputs, turned, semaphores,
):
    cout = bias.shape[1]
    half = volume.shape[3] // 2
    ny = upstream.shape[2]
    copies = Copies(semaphores)
    ins = [copies.start(volume.at[:, 2 + z], field.at[z]) for z in range(2)]
    ups = copies.start(upstream.at[:, 1], inputs)
    table = picks(half, False)
    planes = [lines.at[1], middle, top]
    for z in range(2):
        planes[1 + z][0] = jnp.zeros(top.shape[1:], BF)
        copies.wait(ins[z])
        split_plane(lambda y, z=z: field[z, :, pl.ds(y, 16), :], planes[1 + z], table)
    copies.wait(ups)
    turn_upstream(inputs, turned)
    offset = column(bias)
    for lo, hi in spans(ny, 8):
        block = jnp.concatenate([window(planes, j, 3) for j in range(lo, hi)], 1)
        sums = jnp.dot(full[...], block, preferred_element_type=F32)
        for j in range(lo, hi):
            at = (j - lo) * half
            store_grads(sums[:, at : at + half] + offset, turned[j], grads, j)
    grads[ny] = jnp.zeros(grads.shape[1:], BF)
    terms[...] = plane_terms(planes, grads)


def plane_terms(planes, grads):
    cout = grads.shape[1] // 2
    return weight_terms(
        [
            (
                [plane[1 + 2 * j : 3 + 2 * j] for plane in planes],
                [grads[j, :cout], grads[j + 1, :cout]],
            )
            for j in range(grads.shape[0] - 1)
        ]
    )


def halo_kernel(halo, pre, upstream, full, grads, raw, below):
    half = below.shape[-1]
    cout, ny = full.shape[0], pre.shape[0]
    below[0] = jnp.zeros(below.shape[1:], BF)
    split_plane(lambda y: halo[:, 0, pl.ds(y, 16), :], below, picks(half, False))
    front = full[:, : full.shape[1] // 3]
    for lo, hi in spans(ny, 8):
        block = jnp.concatenate([window([below], j, 3) for j in range(lo, hi)], 1)
        sums = jnp.dot(front, block, preferred_element_type=F32)
        for j in range(lo, hi):
            at = (j - lo) * half
            store_grads(sums[:, at : at + half] + pre[j], upstream[j].astype(F32), grads, j)
            raw[j] = grads[j, :cout, :]
    grads[ny] = jnp.zeros(grads.shape[1:], BF)


def terms_kernel(below, lines, grads, terms_in, kept, sent, packed):
    place = lax.axis_index("slab")
    terms = terms_in[...] + plane_terms([below, lines.at[0], lines.at[1]], grads)
    pack(terms, packed, below.shape[1], grads.shape[1] // 2, place)
    rows = kept.shape[0]
    low, high = packed[:rows], packed[rows:]
    kept[...] = jnp.where(place % 2 == 0, low, high)
    sent[...] = jnp.where(place % 2 == 0, high, low)


def pack(terms, packed, count, cout, place):
    for a in range(3):
        packed[a * count : (a + 1) * count] = terms[(2 * a + 1) * count : (2 * a + 2) * count]
    middle = jnp.concatenate([terms[2 * a * count : (2 * a + 1) * count, :cout] for a in range(3)], 0)
    rows = middle.shape[0] // 2
    packed[3 * count : 3 * count + rows] = jnp.concatenate([middle[:rows], middle[rows:]], 1)
    total = terms[6 * count : 6 * count + 8, :cout]
    high = total.astype(BF).astype(F32)
    both = jnp.concatenate([high, total - high], 1)
    slots = packed.shape[0] - 3 * count - rows
    row = lax.broadcasted_iota(jnp.int32, (slots, 2 * cout), 0)
    packed[3 * count + rows :] = jnp.where(
        row == place, jnp.broadcast_to(both[:1], (slots, 2 * cout)), 0.0
    )


def finish_kernel(mine, got, weight_grad, bias_grad):
    even = lax.axis_index("slab") % 2 == 0
    low = jnp.where(even, mine[...], got[...])
    high = jnp.where(even, got[...], mine[...])
    packed = jnp.concatenate([low, high], 0)
    count = weight_grad.shape[2]
    cout = weight_grad.shape[3]
    for a in range(3):
        block = packed[a * count : (a + 1) * count]
        weight_grad[a, 2] = block[:, :cout]
        weight_grad[a, 0] = block[:, cout:]
    rows = 3 * count // 2
    middle = packed[3 * count : 3 * count + rows]
    middle = jnp.concatenate([middle[:, :cout], middle[:, cout:]], 0)
    for a in range(3):
        weight_grad[a, 1] = middle[a * count : (a + 1) * count]
    total = jnp.sum(packed[3 * count + rows :], axis=0, keepdims=True)
    bias_grad[...] = total[:, :cout] + total[:, cout:]


def back_kernel(z, odd, fresh, aliased, *refs):
    refs = refs[1:] if aliased else refs
    back, grads_in = refs[:2]
    above_in = refs[2 : 2 + odd]
    refs = refs[2 + len(above_in) :]
    total, grads, above, plane, semaphores = refs[:5]
    ny = grads.shape[0] - 1
    cout = grads.shape[1] // 2
    copies = Copies(semaphores)
    loads = []
    for lo, hi in spans(ny, 8):
        top = ny + 1 if hi == ny else hi
        part = [copies.start(grads_in.at[lo:top], grads.at[lo:top])]
        if odd and not fresh:
            part.append(copies.start(above_in[0].at[lo:top], above.at[lo:top]))
        loads.append(part)
    if fresh:
        for j in range(ny):
            value = above_in[0][j]
            above[j, :cout, :] = value
            above[j, cout:, :] = earlier(value.astype(F32)).astype(BF)
        above[ny] = jnp.zeros(above.shape[1:], BF)
    left = jnp.concatenate([back[2], back[0]], 1) if odd else back[1]
    cin = plane.shape[0]
    half = plane.shape[2] // 2
    table = picks(half, True)
    copies.wait(*loads[0])
    for n, (lo, hi) in enumerate(spans(ny, 8)):
        if n + 1 < len(loads):
            copies.wait(*loads[n + 1])
        columns = []
        for j in range(lo, hi):
            parts = [grads[j : j + 2].reshape(-1, half)]
            if odd:
                parts.append(above[j : j + 2].reshape(-1, half))
            columns.append(jnp.concatenate(parts, 0))
        sums = jnp.dot(left, jnp.concatenate(columns, 1), preferred_element_type=F32)
        sums = sums.astype(BF)
        rows = []
        for j in range(hi - lo):
            for py in range(2):
                lanes = slice(j * half, (j + 1) * half)
                even = sums[py * cin : (py + 1) * cin, lanes]
                odds = sums[(2 + py) * cin : (3 + py) * cin, lanes]
                rows.append(jnp.concatenate([even, odds], 1))
        merged = jnp.dot(jnp.concatenate(rows, 0), table, preferred_element_type=F32)
        merged = merged.astype(BF).reshape(2 * (hi - lo), cin, 2 * half)
        plane[:, 2 * lo : 2 * hi, :] = jnp.swapaxes(merged, 0, 1)
        copies.start(plane.at[:, 2 * lo : 2 * hi], total.at[:, z, 2 * lo : 2 * hi])
    copies.wait()


def back_plane(z, total, full, back, grads, above=()):
    cin, depth, height, width = full
    fresh = len(above) > 0 and above[0].shape != grads.shape
    args = [back, grads, *above]
    specs = [VMEM, ANY] + [VMEM if fresh else ANY] * len(above)
    aliased = total is not None
    if aliased:
        args = [total] + args
        specs = [ANY] + specs
    return pl.pallas_call(
        functools.partial(back_kernel, z, len(above) > 0, fresh, aliased),
        in_specs=specs,
        out_specs=ANY,
        out_shape=shape(*full),
        scratch_shapes=[
            pltpu.VMEM(grads.shape, BF),
            pltpu.VMEM(grads.shape if above else (16, 128), BF),
            pltpu.VMEM((cin, height, width), BF),
            pltpu.SemaphoreType.DMA((3 * (height // 16),)),
        ],
        input_output_aliases={0: 0} if aliased else {},
        compiler_params=PARAMS,
        cost_estimate=cost(10**6, 10**3),
    )(*args)


def all_sum(kept, sent, axis, total, above, works):
    peers = lax.axis_size(axis)
    works = list(works)
    swap = [(i, i ^ 1) for i in range(peers)]
    kept, sent, total = lax.optimization_barrier((kept, sent, total))
    got = lax.ppermute(sent, axis, swap)
    total, above = works.pop(0)(total, above)
    got, total = lax.optimization_barrier((got, total))
    value = kept + got
    step = 2
    while step < peers:
        value, total = lax.optimization_barrier((value.astype((BF if 2 * step == peers else F32)), total))
        got = lax.ppermute(value, axis, [(i, i ^ step) for i in range(peers)])
        if works:
            total, above = works.pop(0)(total, above)
        got, total, above = lax.optimization_barrier((got, total, above))
        value = value.astype(F32) + got.astype(F32)
        step *= 2
    for work in works:
        total, above = work(total, above)
    return value, lax.ppermute(value, axis, swap), total


def shifted(x, axis, by):
    peers = lax.axis_size(axis)
    pairs = [(i, i + by) for i in range(peers) if 0 <= i + by < peers]
    return lax.ppermute(x, axis, pairs)


def shards(volume, weights, bias, upstream):
    cin, depth, height, width = volume.shape
    cout = bias.shape[0]
    ny, half = height // 2, width // 2
    rows, count = height + 1, 3 * cin
    halo = shifted(volume[:, depth - 1 :], "slab", 1)
    grads_shape = (ny + 1, 2 * cout, half)
    terms_shape = (6 * count + 16, 2 * cout)
    bias = bias.reshape(1, cout)
    pinned = pltpu.with_memory_space_constraint(volume, pltpu.HBM)
    lines, pre, late, taps, back = pl.pallas_call(
        lower_kernel,
        in_specs=[ANY, ANY, VMEM, ANY],
        out_specs=[VMEM] * 5,
        out_shape=[
            shape(2, rows, count, half),
            shape(ny, cout, half, dtype=F32),
            shape(ny, cout, half),
            shape(cout, 9 * count),
            shape(3, 4 * cin, 4 * cout),
        ],
        scratch_shapes=[
            pltpu.VMEM((2, cin, height, width), BF),
            pltpu.VMEM((cout, ny, half), BF),
            pltpu.VMEM(weights.shape, BF),
            pltpu.SemaphoreType.DMA((4,)),
        ],
        compiler_params=PARAMS,
        cost_estimate=cost(5 * 10**9, 10 * 2**20),
    )(pinned, weights, bias, upstream)
    upper, terms = pl.pallas_call(
        upper_kernel,
        in_specs=[ANY, VMEM, VMEM, VMEM, ANY],
        out_specs=[VMEM] * 2,
        out_shape=[shape(*grads_shape), shape(*terms_shape, dtype=F32)],
        scratch_shapes=[
            pltpu.VMEM((2, cin, height, width), BF),
            pltpu.VMEM((rows, count, half), BF),
            pltpu.VMEM((rows, count, half), BF),
            pltpu.VMEM((cout, ny, half), BF),
            pltpu.VMEM((ny, cout, half), F32),
            pltpu.SemaphoreType.DMA((3,)),
        ],
        compiler_params=PARAMS,
        cost_estimate=cost(6 * 10**9, 10 * 2**20),
    )(pinned, lines, taps, bias, upstream)
    full = volume.shape

    total = back_plane(2, None, full, back, upper)
    total, halo = lax.optimization_barrier((total, halo))
    lower, raw, below = pl.pallas_call(
        halo_kernel,
        in_specs=[VMEM] * 4,
        out_specs=[VMEM] * 3,
        out_shape=[shape(*grads_shape), shape(ny, cout, half), shape(rows, count, half)],
        compiler_params=PARAMS,
        cost_estimate=cost(3 * 10**9, 6 * 2**20),
    )(halo, pre, late, taps)
    slots = (lax.axis_size("slab") + 15) // 16 * 16
    above = shifted(raw, "slab", -1)
    packed_rows = 9 * count // 2 + slots
    kept, sent = pl.pallas_call(
        terms_kernel,
        in_specs=[VMEM] * 4,
        out_specs=[VMEM] * 2,
        out_shape=[shape(packed_rows // 2, 2 * cout, dtype=F32)] * 2,
        scratch_shapes=[pltpu.VMEM((packed_rows, 2 * cout), F32)],
        compiler_params=PARAMS,
        cost_estimate=cost(10**8, 10**5),
    )(below, lines, lower, terms)

    mine, got, total = all_sum(
        kept,
        sent,
        "slab",
        total,
        above,
        [
            lambda t, g: (back_plane(0, t, full, back, lower), g),
            lambda t, g: (back_plane(1, t, full, back, lower, (upper,)), g),
            lambda t, g: (back_plane(3, t, full, back, upper, (g,)), g),
        ],
    )
    weight_grad, bias_grad = pl.pallas_call(
        finish_kernel,
        in_specs=[VMEM] * 2,
        out_specs=[VMEM] * 2,
        out_shape=[shape(3, 3, count, cout, dtype=F32), shape(1, cout, dtype=F32)],
        compiler_params=PARAMS,
    )(mine, got)
    return (
        total,
        weight_grad.reshape(3, 3, 3, cin, cout),
        bias_grad.reshape(cout),
    )


def solution(mesh):
    placed = (
        P(None, ("groups", "slab"), None, None),
        P(),
        P(),
        P(None, ("groups", "slab"), None, None),
    )
    return jax.shard_map(
        shards,
        mesh=mesh,
        in_specs=placed,
        out_specs=(
            P(None, ("groups", "slab"), None, None),
            P("groups", None, None, None, None),
            P("groups"),
        ),
        check_vma=False,
    )
```

```python
import functools

import jax
import jax.numpy as jnp
from jax import lax
from jax.experimental import pallas as pl
from jax.experimental.pallas import tpu as pltpu
from jax.sharding import PartitionSpec as P

BF = jnp.bfloat16
F32 = jnp.float32
VMEM = pl.BlockSpec(memory_space=pltpu.VMEM)
ANY = pl.BlockSpec(memory_space=pl.ANY)
HBM = pl.BlockSpec(memory_space=pltpu.HBM)
SMEM = pl.BlockSpec(memory_space=pltpu.SMEM)
PARAMS = pltpu.CompilerParams(vmem_limit_bytes=40 * 2**20)


def shape(*dims, dtype=BF):
    return jax.ShapeDtypeStruct(dims, dtype)


def cost(flops, size):
    return pl.CostEstimate(flops=flops, bytes_accessed=size, transcendentals=0)


def picks(half, inverse):
    if inverse:
        row = lax.broadcasted_iota(jnp.int32, (2 * half, 2 * half), 0)
        col = lax.broadcasted_iota(jnp.int32, (2 * half, 2 * half), 1)
        hit = jnp.where(row < half, 2 * row, 2 * (row - half) + 1) == col
    else:
        row = lax.broadcasted_iota(jnp.int32, (2 * half, 3 * half), 0)
        col = lax.broadcasted_iota(jnp.int32, (2 * half, 3 * half), 1)
        early = 2 * col - 1
        even = 2 * (col - half)
        odd = 2 * (col - 2 * half) + 1
        hit = jnp.where(col < half, early, jnp.where(col < 2 * half, even, odd)) == row
    return jnp.where(hit, 1.0, 0.0).astype(BF)


def split_plane(read, lines, table):
    rows, channels, half = lines.shape
    channels //= 3

    def step(t, carry):
        block = jnp.swapaxes(read(pl.multiple_of(t * 16, 16)), 0, 1)
        flat = block.reshape(16 * channels, 2 * half)
        taps = jnp.dot(flat, table, preferred_element_type=F32).astype(BF)
        taps = taps.reshape(16, channels, 3 * half)
        for e in range(3):
            lines[pl.ds(1 + t * 16, 16), e * channels : (e + 1) * channels, :] = taps[
                :, :, e * half : (e + 1) * half
            ]
        return carry

    lax.fori_loop(0, (rows - 1) // 16, step, 0, unroll=True)


def turn_upstream(upstream, turned):
    for o in range(0, upstream.shape[0], 8):
        block = upstream[o : o + 8].astype(F32)
        turned[:, o : o + 8, :] = jnp.swapaxes(block, 0, 1).astype(turned.dtype)


def earlier(values):
    cells = values.shape[-1]
    lane = lax.broadcasted_iota(jnp.int32, values.shape, values.ndim - 1)
    return jnp.where(lane == cells - 1, 0.0, pltpu.roll(values, cells - 1, values.ndim - 1))


def store_grads(pre, upstream, grads, j):
    slope = 0.6 + 0.4 * jnp.tanh(0.5 * pre)
    value = (upstream * slope).astype(BF)
    cout = value.shape[0]
    grads[j, :cout, :] = value
    grads[j, cout:, :] = earlier(value.astype(F32)).astype(BF)


def window(planes, j, count):
    parts = [plane[2 * j : 2 * j + count].reshape(-1, plane.shape[-1]) for plane in planes]
    return parts[0] if len(parts) == 1 else jnp.concatenate(parts, 0)


def weight_terms(cells):
    left, right = [], []
    for lines, grads in cells:
        flat = [line.reshape(-1, line.shape[-1]) for line in lines]
        ones = jnp.ones((16, flat[0].shape[-1]), BF)
        left.append(jnp.concatenate(flat + [ones], 0))
        right.append(jnp.concatenate(grads, 0))
    return lax.dot_general(
        jnp.concatenate(left, 1),
        jnp.concatenate(right, 1),
        (((1,), (1,)), ((), ())),
        preferred_element_type=F32,
    )


class Copies:
    def __init__(self, semaphores):
        self.semaphores, self.used, self.pending = semaphores, 0, []

    def start(self, source, target):
        copy = pltpu.make_async_copy(source, target, self.semaphores.at[self.used])
        self.used += 1
        copy.start()
        self.pending.append(copy)
        return copy

    def wait(self, *copies):
        for copy in copies or list(self.pending):
            copy.wait()
            self.pending.remove(copy)


def spans(total, size):
    return [(at, min(at + size, total)) for at in range(0, total, size)]


def edge_kernel(volume, edge, semaphores):
    copies = Copies(semaphores)
    top = volume.shape[1] - 1
    for lo, hi in spans(volume.shape[0], volume.shape[0] // 4):
        copies.start(volume.at[lo:hi, top], edge.at[lo:hi, 0])
    copies.wait()


def column(bias):
    cout = bias.shape[1]
    row = lax.broadcasted_iota(jnp.int32, (cout, cout), 0)
    col = lax.broadcasted_iota(jnp.int32, (cout, cout), 1)
    return jnp.sum(jnp.where(row == col, bias[...], 0.0), axis=1, keepdims=True)


def lower_kernel(
    volume, weights_in, bias, upstream,
    lines, pre, late, full, back,
    field, inputs, weights, semaphores,
):
    cin = volume.shape[0]
    cout = bias.shape[1]
    half = volume.shape[3] // 2
    ny = upstream.shape[2]
    copies = Copies(semaphores)
    kernel = copies.start(weights_in, weights)
    ins = [copies.start(volume.at[:, z], field.at[z]) for z in range(2)]
    ups = copies.start(upstream.at[:, 0], inputs)
    table = picks(half, False)
    copies.wait(kernel)
    for a in range(3):
        for b in range(3):
            block = jnp.concatenate([weights[a, b, e] for e in range(3)], 0)
            at = (3 * a + b) * 3 * cin
            full[:, at : at + 3 * cin] = block.T
    blank = jnp.zeros((cin, cout), BF)
    for a in range(3):
        for px in range(2):
            for py in range(2):
                row = []
                for dy in range(2):
                    for dx in range(2):
                        b, e = py + 1 - 2 * dy, px + 1 - 2 * dx
                        row.append(weights[a, b, e] if b >= 0 and e >= 0 else blank)
                at = (px * 2 + py) * cin
                back[a, at : at + cin, :] = jnp.concatenate(row, 1)
    planes = [lines.at[z] for z in range(2)]
    for z in range(2):
        planes[z][0] = jnp.zeros(planes[z].shape[1:], BF)
        copies.wait(ins[z])
        split_plane(lambda y, z=z: field[z, :, pl.ds(y, 16), :], planes[z], table)
    copies.wait(ups)
    turn_upstream(inputs, late)
    taps = full[:, 9 * cin :]
    offset = column(bias)
    for lo, hi in spans(ny, 8):
        block = jnp.concatenate([window(planes, j, 3) for j in range(lo, hi)], 1)
        sums = jnp.dot(taps, block, preferred_element_type=F32)
        for j in range(lo, hi):
            pre[j] = sums[:, (j - lo) * half : (j - lo + 1) * half] + offset


def upper_kernel(
    volume, lines, full, bias, upstream,
    grads, terms,
    field, middle, top, inputs, turned, semaphores,
):
    cout = bias.shape[1]
    half = volume.shape[3] // 2
    ny = upstream.shape[2]
    copies = Copies(semaphores)
    ins = [copies.start(volume.at[:, 2 + z], field.at[z]) for z in range(2)]
    ups = copies.start(upstream.at[:, 1], inputs)
    table = picks(half, False)
    planes = [lines.at[1], middle, top]
    for z in range(2):
        planes[1 + z][0] = jnp.zeros(top.shape[1:], BF)
        copies.wait(ins[z])
        split_plane(lambda y, z=z: field[z, :, pl.ds(y, 16), :], planes[1 + z], table)
    copies.wait(ups)
    turn_upstream(inputs, turned)
    offset = column(bias)
    for lo, hi in spans(ny, 8):
        block = jnp.concatenate([window(planes, j, 3) for j in range(lo, hi)], 1)
        sums = jnp.dot(full[...], block, preferred_element_type=F32)
        for j in range(lo, hi):
            at = (j - lo) * half
            store_grads(sums[:, at : at + half] + offset, turned[j], grads, j)
    grads[ny] = jnp.zeros(grads.shape[1:], BF)
    terms[...] = plane_terms(planes, grads)


def plane_terms(planes, grads):
    cout = grads.shape[1] // 2
    return weight_terms(
        [
            (
                [plane[1 + 2 * j : 3 + 2 * j] for plane in planes],
                [grads[j, :cout], grads[j + 1, :cout]],
            )
            for j in range(grads.shape[0] - 1)
        ]
    )


def halo_kernel(halo, pre, upstream, full, grads, raw, below):
    half = below.shape[-1]
    cout, ny = full.shape[0], pre.shape[0]
    below[0] = jnp.zeros(below.shape[1:], BF)
    split_plane(lambda y: halo[:, 0, pl.ds(y, 16), :], below, picks(half, False))
    front = full[:, : full.shape[1] // 3]
    for lo, hi in spans(ny, 8):
        block = jnp.concatenate([window([below], j, 3) for j in range(lo, hi)], 1)
        sums = jnp.dot(front, block, preferred_element_type=F32)
        for j in range(lo, hi):
            at = (j - lo) * half
            store_grads(sums[:, at : at + half] + pre[j], upstream[j].astype(F32), grads, j)
            raw[j] = grads[j, :cout, :]
    grads[ny] = jnp.zeros(grads.shape[1:], BF)


def terms_kernel(below, lines, grads, terms_in, kept, sent, packed):
    place = lax.axis_index("slab")
    terms = terms_in[...] + plane_terms([below, lines.at[0], lines.at[1]], grads)
    pack(terms, packed, below.shape[1], grads.shape[1] // 2, place)
    rows = kept.shape[0]
    low, high = packed[:rows], packed[rows:]
    kept[...] = jnp.where(place % 2 == 0, low, high)
    sent[...] = jnp.where(place % 2 == 0, high, low)


def pack(terms, packed, count, cout, place):
    for a in range(3):
        packed[a * count : (a + 1) * count] = terms[(2 * a + 1) * count : (2 * a + 2) * count]
    middle = jnp.concatenate([terms[2 * a * count : (2 * a + 1) * count, :cout] for a in range(3)], 0)
    rows = middle.shape[0] // 2
    packed[3 * count : 3 * count + rows] = jnp.concatenate([middle[:rows], middle[rows:]], 1)
    total = terms[6 * count : 6 * count + 8, :cout]
    high = total.astype(BF).astype(F32)
    both = jnp.concatenate([high, total - high], 1)
    slots = packed.shape[0] - 3 * count - rows
    row = lax.broadcasted_iota(jnp.int32, (slots, 2 * cout), 0)
    packed[3 * count + rows :] = jnp.where(
        row == place, jnp.broadcast_to(both[:1], (slots, 2 * cout)), 0.0
    )


def finish_kernel(mine, got, weight_grad, bias_grad):
    even = lax.axis_index("slab") % 2 == 0
    low = jnp.where(even, mine[...], got[...])
    high = jnp.where(even, got[...], mine[...])
    packed = jnp.concatenate([low, high], 0)
    count = weight_grad.shape[2]
    cout = weight_grad.shape[3]
    for a in range(3):
        block = packed[a * count : (a + 1) * count]
        weight_grad[a, 2] = block[:, :cout]
        weight_grad[a, 0] = block[:, cout:]
    rows = 3 * count // 2
    middle = packed[3 * count : 3 * count + rows]
    middle = jnp.concatenate([middle[:, :cout], middle[:, cout:]], 0)
    for a in range(3):
        weight_grad[a, 1] = middle[a * count : (a + 1) * count]
    total = jnp.sum(packed[3 * count + rows :], axis=0, keepdims=True)
    bias_grad[...] = total[:, :cout] + total[:, cout:]


def back_kernel(z, odd, fresh, aliased, *refs):
    refs = refs[1:] if aliased else refs
    back, grads = refs[:2]
    above_in = refs[2 : 2 + odd]
    total, plane, shifted_above, semaphores = refs[2 + len(above_in) :]
    ny = grads.shape[0] - 1
    cout = grads.shape[1] // 2
    copies = Copies(semaphores)
    above = shifted_above if fresh else above_in[0] if odd else None
    if fresh:
        for j in range(ny):
            value = above_in[0][j]
            above[j, :cout, :] = value
            above[j, cout:, :] = earlier(value.astype(F32)).astype(BF)
        above[ny] = jnp.zeros(above.shape[1:], BF)
    left = jnp.concatenate([back[2], back[0]], 1) if odd else back[1]
    cin = plane.shape[0]
    half = plane.shape[2] // 2
    table = picks(half, True)
    for lo, hi in spans(ny, 8):
        columns = []
        for j in range(lo, hi):
            parts = [grads[j : j + 2].reshape(-1, half)]
            if odd:
                parts.append(above[j : j + 2].reshape(-1, half))
            columns.append(jnp.concatenate(parts, 0))
        sums = jnp.dot(left, jnp.concatenate(columns, 1), preferred_element_type=F32)
        sums = sums.astype(BF)
        rows = []
        for j in range(hi - lo):
            for py in range(2):
                lanes = slice(j * half, (j + 1) * half)
                even = sums[py * cin : (py + 1) * cin, lanes]
                odds = sums[(2 + py) * cin : (3 + py) * cin, lanes]
                rows.append(jnp.concatenate([even, odds], 1))
        merged = jnp.dot(jnp.concatenate(rows, 0), table, preferred_element_type=F32)
        merged = merged.astype(BF).reshape(2 * (hi - lo), cin, 2 * half)
        plane[:, 2 * lo : 2 * hi, :] = jnp.swapaxes(merged, 0, 1)
        copies.start(plane.at[:, 2 * lo : 2 * hi], total.at[:, z, 2 * lo : 2 * hi])
    copies.wait()


def back_plane(z, total, full, back, grads, above=()):
    cin, depth, height, width = full
    fresh = len(above) > 0 and above[0].shape != grads.shape
    args = [back, grads, *above]
    specs = [VMEM] * len(args)
    aliased = total is not None
    if aliased:
        args = [total] + args
        specs = [ANY] + specs
    return pl.pallas_call(
        functools.partial(back_kernel, z, len(above) > 0, fresh, aliased),
        in_specs=specs,
        out_specs=ANY,
        out_shape=shape(*full),
        scratch_shapes=[
            pltpu.VMEM((cin, height, width), BF),
            pltpu.VMEM(grads.shape if fresh else (16, 128), BF),
            pltpu.SemaphoreType.DMA((height // 16,)),
        ],
        input_output_aliases={0: 0} if aliased else {},
        compiler_params=PARAMS,
        cost_estimate=cost(10**6, 10**3),
    )(*args)


def all_sum(kept, sent, axis, total, above, works):
    peers = lax.axis_size(axis)
    works = list(works)
    swap = [(i, i ^ 1) for i in range(peers)]
    kept, sent, total = lax.optimization_barrier((kept, sent, total))
    got = lax.ppermute(sent, axis, swap)
    total, above = works.pop(0)(total, above)
    got, total = lax.optimization_barrier((got, total))
    value = kept + got
    step = 2
    while step < peers:
        value, total = lax.optimization_barrier((value.astype((BF if 2 * step == peers else F32)), total))
        got = lax.ppermute(value, axis, [(i, i ^ step) for i in range(peers)])
        if works:
            total, above = works.pop(0)(total, above)
        got, total, above = lax.optimization_barrier((got, total, above))
        value = value.astype(F32) + got.astype(F32)
        step *= 2
    for work in works:
        total, above = work(total, above)
    return value, lax.ppermute(value, axis, swap), total


def shifted(x, axis, by):
    peers = lax.axis_size(axis)
    pairs = [(i, i + by) for i in range(peers) if 0 <= i + by < peers]
    return lax.ppermute(x, axis, pairs)


def shards(volume, weights, bias, upstream):
    cin, depth, height, width = volume.shape
    cout = bias.shape[0]
    ny, half = height // 2, width // 2
    rows, count = height + 1, 3 * cin
    pinned = pltpu.with_memory_space_constraint(volume, pltpu.HBM)
    edge = pl.pallas_call(
        edge_kernel,
        in_specs=[ANY],
        out_specs=VMEM,
        out_shape=shape(cin, 1, height, width),
        scratch_shapes=[pltpu.SemaphoreType.DMA((4,))],
        compiler_params=PARAMS,
        cost_estimate=cost(0, 3 * 2**20),
    )(pinned)
    halo = shifted(edge, "slab", 1)
    grads_shape = (ny + 1, 2 * cout, half)
    terms_shape = (6 * count + 16, 2 * cout)
    bias = bias.reshape(1, cout)
    lines, pre, late, taps, back = pl.pallas_call(
        lower_kernel,
        in_specs=[ANY, ANY, VMEM, ANY],
        out_specs=[VMEM] * 5,
        out_shape=[
            shape(2, rows, count, half),
            shape(ny, cout, half, dtype=F32),
            shape(ny, cout, half),
            shape(cout, 9 * count),
            shape(3, 4 * cin, 4 * cout),
        ],
        scratch_shapes=[
            pltpu.VMEM((2, cin, height, width), BF),
            pltpu.VMEM((cout, ny, half), BF),
            pltpu.VMEM(weights.shape, BF),
            pltpu.SemaphoreType.DMA((4,)),
        ],
        compiler_params=PARAMS,
        cost_estimate=cost(5 * 10**9, 10 * 2**20),
    )(pinned, weights, bias, upstream)
    upper, terms = pl.pallas_call(
        upper_kernel,
        in_specs=[ANY, VMEM, VMEM, VMEM, ANY],
        out_specs=[VMEM] * 2,
        out_shape=[shape(*grads_shape), shape(*terms_shape, dtype=F32)],
        scratch_shapes=[
            pltpu.VMEM((2, cin, height, width), BF),
            pltpu.VMEM((rows, count, half), BF),
            pltpu.VMEM((rows, count, half), BF),
            pltpu.VMEM((cout, ny, half), BF),
            pltpu.VMEM((ny, cout, half), F32),
            pltpu.SemaphoreType.DMA((3,)),
        ],
        compiler_params=PARAMS,
        cost_estimate=cost(6 * 10**9, 10 * 2**20),
    )(pinned, lines, taps, bias, upstream)
    full = volume.shape

    total = back_plane(2, None, full, back, upper)
    total, halo = lax.optimization_barrier((total, halo))
    lower, raw, below = pl.pallas_call(
        halo_kernel,
        in_specs=[VMEM] * 4,
        out_specs=[VMEM] * 3,
        out_shape=[shape(*grads_shape), shape(ny, cout, half), shape(rows, count, half)],
        compiler_params=PARAMS,
        cost_estimate=cost(3 * 10**9, 6 * 2**20),
    )(halo, pre, late, taps)
    slots = (lax.axis_size("slab") + 15) // 16 * 16
    above = shifted(raw, "slab", -1)
    packed_rows = 9 * count // 2 + slots
    kept, sent = pl.pallas_call(
        terms_kernel,
        in_specs=[VMEM] * 4,
        out_specs=[VMEM] * 2,
        out_shape=[shape(packed_rows // 2, 2 * cout, dtype=F32)] * 2,
        scratch_shapes=[pltpu.VMEM((packed_rows, 2 * cout), F32)],
        compiler_params=PARAMS,
        cost_estimate=cost(10**8, 10**5),
    )(below, lines, lower, terms)

    mine, got, total = all_sum(
        kept,
        sent,
        "slab",
        total,
        above,
        [
            lambda t, g: (back_plane(0, t, full, back, lower), g),
            lambda t, g: (back_plane(1, t, full, back, lower, (upper,)), g),
            lambda t, g: (back_plane(3, t, full, back, upper, (g,)), g),
        ],
    )
    weight_grad, bias_grad = pl.pallas_call(
        finish_kernel,
        in_specs=[VMEM] * 2,
        out_specs=[VMEM] * 2,
        out_shape=[shape(3, 3, count, cout, dtype=F32), shape(1, cout, dtype=F32)],
        compiler_params=PARAMS,
    )(mine, got)
    return (
        total,
        weight_grad.reshape(3, 3, 3, cin, cout),
        bias_grad.reshape(cout),
    )


def solution(mesh):
    placed = (
        P(None, ("groups", "slab"), None, None),
        P(),
        P(),
        P(None, ("groups", "slab"), None, None),
    )
    return jax.shard_map(
        shards,
        mesh=mesh,
        in_specs=placed,
        out_specs=(
            P(None, ("groups", "slab"), None, None),
            P("groups", None, None, None, None),
            P("groups"),
        ),
        check_vma=False,
    )
```

```python
import functools

import jax
import jax.numpy as jnp
from jax import lax
from jax.experimental import pallas as pl
from jax.experimental.pallas import tpu as pltpu
from jax.sharding import PartitionSpec as P

BF = jnp.bfloat16
F32 = jnp.float32
VMEM = pl.BlockSpec(memory_space=pltpu.VMEM)
ANY = pl.BlockSpec(memory_space=pl.ANY)
HBM = pl.BlockSpec(memory_space=pltpu.HBM)
SMEM = pl.BlockSpec(memory_space=pltpu.SMEM)
PARAMS = pltpu.CompilerParams(vmem_limit_bytes=40 * 2**20)


def shape(*dims, dtype=BF):
    return jax.ShapeDtypeStruct(dims, dtype)


def cost(flops, size):
    return pl.CostEstimate(flops=flops, bytes_accessed=size, transcendentals=0)


def picks(half, inverse):
    if inverse:
        row = lax.broadcasted_iota(jnp.int32, (2 * half, 2 * half), 0)
        col = lax.broadcasted_iota(jnp.int32, (2 * half, 2 * half), 1)
        hit = jnp.where(row < half, 2 * row, 2 * (row - half) + 1) == col
    else:
        row = lax.broadcasted_iota(jnp.int32, (2 * half, 3 * half), 0)
        col = lax.broadcasted_iota(jnp.int32, (2 * half, 3 * half), 1)
        early = 2 * col - 1
        even = 2 * (col - half)
        odd = 2 * (col - 2 * half) + 1
        hit = jnp.where(col < half, early, jnp.where(col < 2 * half, even, odd)) == row
    return jnp.where(hit, 1.0, 0.0).astype(BF)


def split_plane(read, lines, table):
    rows, channels, half = lines.shape
    channels //= 3

    def step(t, carry):
        block = jnp.swapaxes(read(pl.multiple_of(t * 16, 16)), 0, 1)
        flat = block.reshape(16 * channels, 2 * half)
        taps = jnp.dot(flat, table, preferred_element_type=F32).astype(BF)
        taps = taps.reshape(16, channels, 3 * half)
        for e in range(3):
            lines[pl.ds(1 + t * 16, 16), e * channels : (e + 1) * channels, :] = taps[
                :, :, e * half : (e + 1) * half
            ]
        return carry

    lax.fori_loop(0, (rows - 1) // 16, step, 0, unroll=True)


def turn_upstream(upstream, turned):
    for o in range(0, upstream.shape[0], 8):
        block = upstream[o : o + 8].astype(F32)
        turned[:, o : o + 8, :] = jnp.swapaxes(block, 0, 1).astype(turned.dtype)


def earlier(values):
    cells = values.shape[-1]
    lane = lax.broadcasted_iota(jnp.int32, values.shape, values.ndim - 1)
    return jnp.where(lane == cells - 1, 0.0, pltpu.roll(values, cells - 1, values.ndim - 1))


def store_grads(pre, upstream, grads, j):
    slope = 0.6 + 0.4 * jnp.tanh(0.5 * pre)
    value = (upstream * slope).astype(BF)
    cout = value.shape[0]
    grads[j, :cout, :] = value
    grads[j, cout:, :] = earlier(value.astype(F32)).astype(BF)


def window(planes, j, count):
    parts = [plane[2 * j : 2 * j + count].reshape(-1, plane.shape[-1]) for plane in planes]
    return parts[0] if len(parts) == 1 else jnp.concatenate(parts, 0)


def weight_terms(cells):
    left, right = [], []
    for lines, grads in cells:
        flat = [line.reshape(-1, line.shape[-1]) for line in lines]
        ones = jnp.ones((16, flat[0].shape[-1]), BF)
        left.append(jnp.concatenate(flat + [ones], 0))
        right.append(jnp.concatenate(grads, 0))
    return lax.dot_general(
        jnp.concatenate(left, 1),
        jnp.concatenate(right, 1),
        (((1,), (1,)), ((), ())),
        preferred_element_type=F32,
    )


class Copies:
    def __init__(self, semaphores):
        self.semaphores, self.used, self.pending = semaphores, 0, []

    def start(self, source, target):
        copy = pltpu.make_async_copy(source, target, self.semaphores.at[self.used])
        self.used += 1
        copy.start()
        self.pending.append(copy)
        return copy

    def wait(self, *copies):
        for copy in copies or list(self.pending):
            copy.wait()
            self.pending.remove(copy)


def spans(total, size):
    return [(at, min(at + size, total)) for at in range(0, total, size)]


def edge_kernel(volume, edge, semaphores):
    copies = Copies(semaphores)
    top = volume.shape[1] - 1
    for lo, hi in spans(volume.shape[0], volume.shape[0] // 4):
        copies.start(volume.at[lo:hi, top], edge.at[lo:hi, 0])
    copies.wait()


def column(bias):
    cout = bias.shape[1]
    row = lax.broadcasted_iota(jnp.int32, (cout, cout), 0)
    col = lax.broadcasted_iota(jnp.int32, (cout, cout), 1)
    return jnp.sum(jnp.where(row == col, bias[...], 0.0), axis=1, keepdims=True)


def lower_kernel(
    volume, weights_in, bias, upstream,
    lines, pre, late, full, back,
    field, inputs, weights, semaphores,
):
    cin = volume.shape[0]
    cout = bias.shape[1]
    half = volume.shape[3] // 2
    ny = upstream.shape[2]
    copies = Copies(semaphores)
    kernel = copies.start(weights_in, weights)
    ins = [copies.start(volume.at[:, z], field.at[z]) for z in range(2)]
    ups = copies.start(upstream.at[:, 0], inputs)
    table = picks(half, False)
    copies.wait(kernel)
    for a in range(3):
        for b in range(3):
            block = jnp.concatenate([weights[a, b, e] for e in range(3)], 0)
            at = (3 * a + b) * 3 * cin
            full[:, at : at + 3 * cin] = block.T
    blank = jnp.zeros((cin, cout), BF)
    for a in range(3):
        for px in range(2):
            for py in range(2):
                row = []
                for dy in range(2):
                    for dx in range(2):
                        b, e = py + 1 - 2 * dy, px + 1 - 2 * dx
                        row.append(weights[a, b, e] if b >= 0 and e >= 0 else blank)
                at = (px * 2 + py) * cin
                back[a, at : at + cin, :] = jnp.concatenate(row, 1)
    planes = [lines.at[z] for z in range(2)]
    for z in range(2):
        planes[z][0] = jnp.zeros(planes[z].shape[1:], BF)
        copies.wait(ins[z])
        split_plane(lambda y, z=z: field[z, :, pl.ds(y, 16), :], planes[z], table)
    copies.wait(ups)
    turn_upstream(inputs, late)
    taps = full[:, 9 * cin :]
    offset = column(bias)
    for lo, hi in spans(ny, 8):
        block = jnp.concatenate([window(planes, j, 3) for j in range(lo, hi)], 1)
        sums = jnp.dot(taps, block, preferred_element_type=F32)
        for j in range(lo, hi):
            pre[j] = sums[:, (j - lo) * half : (j - lo + 1) * half] + offset


def upper_kernel(
    volume, lines, full, bias, upstream,
    grads, terms,
    field, middle, top, inputs, turned, semaphores,
):
    cout = bias.shape[1]
    half = volume.shape[3] // 2
    ny = upstream.shape[2]
    copies = Copies(semaphores)
    ins = [copies.start(volume.at[:, 2 + z], field.at[z]) for z in range(2)]
    ups = copies.start(upstream.at[:, 1], inputs)
    table = picks(half, False)
    planes = [lines.at[1], middle, top]
    for z in range(2):
        planes[1 + z][0] = jnp.zeros(top.shape[1:], BF)
        copies.wait(ins[z])
        split_plane(lambda y, z=z: field[z, :, pl.ds(y, 16), :], planes[1 + z], table)
    copies.wait(ups)
    turn_upstream(inputs, turned)
    offset = column(bias)
    for lo, hi in spans(ny, 8):
        block = jnp.concatenate([window(planes, j, 3) for j in range(lo, hi)], 1)
        sums = jnp.dot(full[...], block, preferred_element_type=F32)
        for j in range(lo, hi):
            at = (j - lo) * half
            store_grads(sums[:, at : at + half] + offset, turned[j], grads, j)
    grads[ny] = jnp.zeros(grads.shape[1:], BF)
    terms[...] = plane_terms(planes, grads)


def plane_terms(planes, grads):
    cout = grads.shape[1] // 2
    return weight_terms(
        [
            (
                [plane[1 + 2 * j : 3 + 2 * j] for plane in planes],
                [grads[j, :cout], grads[j + 1, :cout]],
            )
            for j in range(grads.shape[0] - 1)
        ]
    )


def halo_kernel(halo, pre, upstream, full, grads, raw, below):
    half = below.shape[-1]
    cout, ny = full.shape[0], pre.shape[0]
    below[0] = jnp.zeros(below.shape[1:], BF)
    split_plane(lambda y: halo[:, 0, pl.ds(y, 16), :], below, picks(half, False))
    front = full[:, : full.shape[1] // 3]
    for lo, hi in spans(ny, 8):
        block = jnp.concatenate([window([below], j, 3) for j in range(lo, hi)], 1)
        sums = jnp.dot(front, block, preferred_element_type=F32)
        for j in range(lo, hi):
            at = (j - lo) * half
            store_grads(sums[:, at : at + half] + pre[j], upstream[j].astype(F32), grads, j)
            raw[j] = grads[j, :cout, :]
    grads[ny] = jnp.zeros(grads.shape[1:], BF)


def terms_kernel(below, lines, grads, terms_in, kept, sent, packed):
    place = lax.axis_index("slab")
    terms = terms_in[...] + plane_terms([below, lines.at[0], lines.at[1]], grads)
    pack(terms, packed, below.shape[1], grads.shape[1] // 2, place)
    rows = kept.shape[0]
    low, high = packed[:rows], packed[rows:]
    kept[...] = jnp.where(place % 2 == 0, low, high)
    sent[...] = jnp.where(place % 2 == 0, high, low)


def pack(terms, packed, count, cout, place):
    for a in range(3):
        packed[a * count : (a + 1) * count] = terms[(2 * a + 1) * count : (2 * a + 2) * count]
    middle = jnp.concatenate([terms[2 * a * count : (2 * a + 1) * count, :cout] for a in range(3)], 0)
    rows = middle.shape[0] // 2
    packed[3 * count : 3 * count + rows] = jnp.concatenate([middle[:rows], middle[rows:]], 1)
    total = terms[6 * count : 6 * count + 8, :cout]
    high = total.astype(BF).astype(F32)
    both = jnp.concatenate([high, total - high], 1)
    slots = packed.shape[0] - 3 * count - rows
    row = lax.broadcasted_iota(jnp.int32, (slots, 2 * cout), 0)
    packed[3 * count + rows :] = jnp.where(
        row == place, jnp.broadcast_to(both[:1], (slots, 2 * cout)), 0.0
    )


def finish_kernel(mine, got, weight_grad, bias_grad):
    even = lax.axis_index("slab") % 2 == 0
    low = jnp.where(even, mine[...], got[...])
    high = jnp.where(even, got[...], mine[...])
    packed = jnp.concatenate([low, high], 0)
    count = weight_grad.shape[2]
    cout = weight_grad.shape[3]
    for a in range(3):
        block = packed[a * count : (a + 1) * count]
        weight_grad[a, 2] = block[:, :cout]
        weight_grad[a, 0] = block[:, cout:]
    rows = 3 * count // 2
    middle = packed[3 * count : 3 * count + rows]
    middle = jnp.concatenate([middle[:, :cout], middle[:, cout:]], 0)
    for a in range(3):
        weight_grad[a, 1] = middle[a * count : (a + 1) * count]
    total = jnp.sum(packed[3 * count + rows :], axis=0, keepdims=True)
    bias_grad[...] = total[:, :cout] + total[:, cout:]


def back_kernel(z, odd, fresh, aliased, *refs):
    refs = refs[1:] if aliased else refs
    back, grads = refs[:2]
    above_in = refs[2 : 2 + odd]
    total, plane, shifted_above, semaphores = refs[2 + len(above_in) :]
    ny = grads.shape[0] - 1
    cout = grads.shape[1] // 2
    copies = Copies(semaphores)
    above = shifted_above if fresh else above_in[0] if odd else None
    if fresh:
        for j in range(ny):
            value = above_in[0][j]
            above[j, :cout, :] = value
            above[j, cout:, :] = earlier(value.astype(F32)).astype(BF)
        above[ny] = jnp.zeros(above.shape[1:], BF)
    left = jnp.concatenate([back[2], back[0]], 1) if odd else back[1]
    cin = plane.shape[0]
    half = plane.shape[2] // 2
    table = picks(half, True)
    for lo, hi in spans(ny, 8):
        columns = []
        for j in range(lo, hi):
            parts = [grads[j : j + 2].reshape(-1, half)]
            if odd:
                parts.append(above[j : j + 2].reshape(-1, half))
            columns.append(jnp.concatenate(parts, 0))
        sums = jnp.dot(left, jnp.concatenate(columns, 1), preferred_element_type=F32)
        sums = sums.astype(BF)
        rows = []
        for j in range(hi - lo):
            for py in range(2):
                lanes = slice(j * half, (j + 1) * half)
                even = sums[py * cin : (py + 1) * cin, lanes]
                odds = sums[(2 + py) * cin : (3 + py) * cin, lanes]
                rows.append(jnp.concatenate([even, odds], 1))
        merged = jnp.dot(jnp.concatenate(rows, 0), table, preferred_element_type=F32)
        merged = merged.astype(BF).reshape(2 * (hi - lo), cin, 2 * half)
        plane[:, 2 * lo : 2 * hi, :] = jnp.swapaxes(merged, 0, 1)
        copies.start(plane.at[:, 2 * lo : 2 * hi], total.at[:, z, 2 * lo : 2 * hi])
    copies.wait()


def back_plane(z, total, full, back, grads, above=()):
    cin, depth, height, width = full
    fresh = len(above) > 0 and above[0].shape != grads.shape
    args = [back, grads, *above]
    specs = [VMEM] * len(args)
    aliased = total is not None
    if aliased:
        args = [total] + args
        specs = [ANY] + specs
    return pl.pallas_call(
        functools.partial(back_kernel, z, len(above) > 0, fresh, aliased),
        in_specs=specs,
        out_specs=ANY,
        out_shape=shape(*full),
        scratch_shapes=[
            pltpu.VMEM((cin, height, width), BF),
            pltpu.VMEM(grads.shape if fresh else (16, 128), BF),
            pltpu.SemaphoreType.DMA((height // 16,)),
        ],
        input_output_aliases={0: 0} if aliased else {},
        compiler_params=PARAMS,
        cost_estimate=cost(10**6, 10**3),
    )(*args)


def all_sum(kept, sent, axis, total, above, works):
    peers = lax.axis_size(axis)
    works = list(works)
    swap = [(i, i ^ 1) for i in range(peers)]
    kept, sent, total = lax.optimization_barrier((kept, sent, total))
    got = lax.ppermute(sent, axis, swap)
    total, above = works.pop(0)(total, above)
    got, total = lax.optimization_barrier((got, total))
    value = kept + got
    step = 2
    while step < peers:
        value, total = lax.optimization_barrier((value.astype((BF if 4 * step >= peers else F32)), total))
        got = lax.ppermute(value, axis, [(i, i ^ step) for i in range(peers)])
        if works:
            total, above = works.pop(0)(total, above)
        got, total, above = lax.optimization_barrier((got, total, above))
        value = value.astype(F32) + got.astype(F32)
        step *= 2
    for work in works:
        total, above = work(total, above)
    return value, lax.ppermute(value, axis, swap), total


def shifted(x, axis, by):
    peers = lax.axis_size(axis)
    pairs = [(i, i + by) for i in range(peers) if 0 <= i + by < peers]
    return lax.ppermute(x, axis, pairs)


def shards(volume, weights, bias, upstream):
    cin, depth, height, width = volume.shape
    cout = bias.shape[0]
    ny, half = height // 2, width // 2
    rows, count = height + 1, 3 * cin
    pinned = pltpu.with_memory_space_constraint(volume, pltpu.HBM)
    edge = pl.pallas_call(
        edge_kernel,
        in_specs=[ANY],
        out_specs=VMEM,
        out_shape=shape(cin, 1, height, width),
        scratch_shapes=[pltpu.SemaphoreType.DMA((4,))],
        compiler_params=PARAMS,
        cost_estimate=cost(0, 3 * 2**20),
    )(pinned)
    halo = shifted(edge, "slab", 1)
    grads_shape = (ny + 1, 2 * cout, half)
    terms_shape = (6 * count + 16, 2 * cout)
    bias = bias.reshape(1, cout)
    lines, pre, late, taps, back = pl.pallas_call(
        lower_kernel,
        in_specs=[ANY, ANY, VMEM, ANY],
        out_specs=[VMEM] * 5,
        out_shape=[
            shape(2, rows, count, half),
            shape(ny, cout, half, dtype=F32),
            shape(ny, cout, half),
            shape(cout, 9 * count),
            shape(3, 4 * cin, 4 * cout),
        ],
        scratch_shapes=[
            pltpu.VMEM((2, cin, height, width), BF),
            pltpu.VMEM((cout, ny, half), BF),
            pltpu.VMEM(weights.shape, BF),
            pltpu.SemaphoreType.DMA((4,)),
        ],
        compiler_params=PARAMS,
        cost_estimate=cost(5 * 10**9, 10 * 2**20),
    )(pinned, weights, bias, upstream)
    upper, terms = pl.pallas_call(
        upper_kernel,
        in_specs=[ANY, VMEM, VMEM, VMEM, ANY],
        out_specs=[VMEM] * 2,
        out_shape=[shape(*grads_shape), shape(*terms_shape, dtype=F32)],
        scratch_shapes=[
            pltpu.VMEM((2, cin, height, width), BF),
            pltpu.VMEM((rows, count, half), BF),
            pltpu.VMEM((rows, count, half), BF),
            pltpu.VMEM((cout, ny, half), BF),
            pltpu.VMEM((ny, cout, half), F32),
            pltpu.SemaphoreType.DMA((3,)),
        ],
        compiler_params=PARAMS,
        cost_estimate=cost(6 * 10**9, 10 * 2**20),
    )(pinned, lines, taps, bias, upstream)
    full = volume.shape

    total = back_plane(2, None, full, back, upper)
    total, halo = lax.optimization_barrier((total, halo))
    lower, raw, below = pl.pallas_call(
        halo_kernel,
        in_specs=[VMEM] * 4,
        out_specs=[VMEM] * 3,
        out_shape=[shape(*grads_shape), shape(ny, cout, half), shape(rows, count, half)],
        compiler_params=PARAMS,
        cost_estimate=cost(3 * 10**9, 6 * 2**20),
    )(halo, pre, late, taps)
    slots = (lax.axis_size("slab") + 15) // 16 * 16
    above = shifted(raw, "slab", -1)
    packed_rows = 9 * count // 2 + slots
    kept, sent = pl.pallas_call(
        terms_kernel,
        in_specs=[VMEM] * 4,
        out_specs=[VMEM] * 2,
        out_shape=[shape(packed_rows // 2, 2 * cout, dtype=F32)] * 2,
        scratch_shapes=[pltpu.VMEM((packed_rows, 2 * cout), F32)],
        compiler_params=PARAMS,
        cost_estimate=cost(10**8, 10**5),
    )(below, lines, lower, terms)

    mine, got, total = all_sum(
        kept,
        sent,
        "slab",
        total,
        above,
        [
            lambda t, g: (back_plane(0, t, full, back, lower), g),
            lambda t, g: (back_plane(1, t, full, back, lower, (upper,)), g),
            lambda t, g: (back_plane(3, t, full, back, upper, (g,)), g),
        ],
    )
    weight_grad, bias_grad = pl.pallas_call(
        finish_kernel,
        in_specs=[VMEM] * 2,
        out_specs=[VMEM] * 2,
        out_shape=[shape(3, 3, count, cout, dtype=F32), shape(1, cout, dtype=F32)],
        compiler_params=PARAMS,
    )(mine, got)
    return (
        total,
        weight_grad.reshape(3, 3, 3, cin, cout),
        bias_grad.reshape(cout),
    )


def solution(mesh):
    placed = (
        P(None, ("groups", "slab"), None, None),
        P(),
        P(),
        P(None, ("groups", "slab"), None, None),
    )
    return jax.shard_map(
        shards,
        mesh=mesh,
        in_specs=placed,
        out_specs=(
            P(None, ("groups", "slab"), None, None),
            P("groups", None, None, None, None),
            P("groups"),
        ),
        check_vma=False,
    )
```
